32 devices in a mesh: groups: 2 (over x), wide: 16 (over z, y, core).
Axes of the slice: x: 2, y: 2, z: 4, core: 2. Of those that a mesh axis runs over, the one named last changes fastest.
Arguments:
- prefill_blocks: bfloat16 [2048, 128, 576], P(('groups', 'wide')), parts along dimension 0, may hold values from -8 to 8
- block_owner: int32 [2048], P(('groups', 'wide')), parts along dimension 0, may hold values from -1 to 15, as said below
- block_position: int32 [2048], P(('groups', 'wide')), parts along dimension 0, may hold values from 0 to 63, as said below
- cache_len: int32 [32], P(('groups', 'wide')), parts along dimension 0, may hold values from 1 to 8192, as said below
- query_nope: bfloat16 [32, 3, 128, 128], P('groups', None, 'wide'), parts along dimension 0, may hold values from -6 to 6
- query_rope: bfloat16 [32, 3, 128, 64], P('groups', None, 'wide'), parts along dimension 0, may hold values from -256 to 256
- w_uk: bfloat16 [128, 128, 512], P('wide'), may hold values from -0.5 to 0.5
- w_uv: bfloat16 [128, 512, 128], P('wide'), may hold values from -2 to 2
- w_o: bfloat16 [16384, 7168], P('wide'), may hold values from -0.046875 to 0.046875
- new_latent: bfloat16 [32, 3, 576], P(('groups', 'wide')), parts along dimension 0, may hold values from -6 to 6
Outputs:
- layer_out: bfloat16 [32, 3, 7168], P(('groups', 'wide')), parts along dimension 0
The draws below stay inside these ranges and needn't reach their ends.
There are 2 independent parts, one for each index of `groups`. The reference program is written for one: setup_inputs(seed, part) draws one part's arguments, and reference() takes and returns one part's arrays. A program takes and returns all parts, laid end to end along the dimension named above; an argument that names none is the same for every part. Nothing has to cross between parts.
Inputs may be any that keep to these rules, and one draw needn't show every extreme that they name: `block_owner`: device i of wide owns request i. No device sends more than 4 blocks to one owner, and some device sends exactly 4 to some owner. Owner r receives 64 // 2 to 64 blocks (at least 1), with block_position 0 up to their count less one, each once; some owner receives 64. `block_position`: 0 on empty slots. `cache_len`: all blocks of a request but its last are full; the last holds 1 to 128 live tokens.
All inputs are finite; a program needn't handle non-finite values.
Results may differ from the reference program's by a relative error of at most 0.0095.
Values may be sent and summed in bfloat16 or wider, within the bound.
A program may use at most 128 MiB of HBM per device.

```python
import jax
import jax.numpy as jnp
from jax import lax

D = 7168
HEADS = 128
KVL = 512
ROPE = 64
NOPE = 128
VD = 128
BLK = 128
STEPS = 3
PRE_BLK = 64
REQUESTS = 16
SLOTS = 1024
N_WIDE = 16


def layout(key):
    key = jax.random.fold_in(key, 101)
    key_perm, key_len, key_busy, key_tail, key_order = jax.random.split(key, 5)
    shuffled = jax.random.permutation(key_perm, N_WIDE)
    peer_ids = jnp.arange(N_WIDE)
    halfway = N_WIDE // 2
    offsets = jnp.where(peer_ids == 0, halfway, jnp.where(shuffled == halfway, shuffled[0], shuffled))
    owners = jnp.arange(N_WIDE)
    counts = jax.random.randint(key_len, (N_WIDE,), max(PRE_BLK // 2, 1), PRE_BLK + 1)
    busiest = jax.random.randint(key_busy, (), 0, N_WIDE)
    counts = jnp.where(owners == busiest, PRE_BLK, counts)
    tail_len = jax.random.randint(key_tail, (N_WIDE,), 1, BLK + 1)
    tail_len = jnp.where(owners == busiest, BLK, tail_len)
    cache_tokens = (counts - 1) * BLK + tail_len
    shuffle = jax.vmap(lambda one_key: jax.random.permutation(one_key, PRE_BLK))(jax.random.split(key_order, N_WIDE))
    slot_ids = jnp.arange(PRE_BLK)
    usable = slot_ids[None, :] < counts[:, None]
    before = (shuffle[:, None, :] < shuffle[:, :, None]) & usable[:, None, :]
    placement_rank = jnp.sum(before.astype(jnp.int32), axis=2)
    destination = (owners[:, None] + offsets[slot_ids % N_WIDE][None, :]) % N_WIDE
    is_live = slot_ids[None, :] < counts[destination]
    owner_list = jnp.where(is_live, destination, -1).reshape(-1)
    position = jnp.where(is_live, placement_rank[destination, slot_ids[None, :]], 0).reshape(-1)
    return (owner_list.astype(jnp.int32), position.astype(jnp.int32), cache_tokens.astype(jnp.int32))


def latents_for(key, indices):

    def one_block(index):
        block_key = jax.random.fold_in(jax.random.fold_in(key, 202), index)
        key_normal = jax.random.fold_in(block_key, 0)
        shape = (BLK, KVL + ROPE)
        base_draw = jnp.clip(jax.random.normal(key_normal, shape, jnp.float32), -6.0, 6.0)
        rope_second = base_draw[1, KVL:]
        return base_draw.at[1, KVL:].set(rope_second)
    return jax.vmap(one_block)(indices)


def draw_prefill_blocks(key, part):
    values = latents_for(key, jnp.arange(SLOTS))
    return values.astype(jnp.bfloat16)


def draw_block_owner(key, part):
    owner_list, position, cache_tokens = layout(key)
    return owner_list


def draw_block_position(key, part):
    owner_list, position, cache_tokens = layout(key)
    return position


def draw_cache_len(key, part):
    owner_list, position, cache_tokens = layout(key)
    return cache_tokens


def draw_query_rope(key, part):
    shape = (REQUESTS, STEPS, HEADS, ROPE)
    own_key = jax.random.fold_in(key, 7)
    result = jnp.clip(jax.random.normal(own_key, shape, jnp.float32), -6.0, 6.0)
    return result.astype(jnp.bfloat16)


def block_levels(key, shape, pieces, least, top_value):
    def one(axis_at, parts):
        steps = jax.random.uniform(jax.random.fold_in(jax.random.fold_in(key, 6), axis_at), (parts,), jnp.float32, least / len(pieces), top_value / len(pieces))
        return jnp.repeat(jnp.exp(steps), shape[axis_at] // parts).reshape((-1,) + (1,) * (len(shape) - axis_at - 1))

    factor_of = one(*pieces[0])
    for cut in pieces[1:]:
        factor_of = factor_of * one(*cut)
    return factor_of


def gaussian(rng, shape, spread, most, cuts=(), held_as=jnp.bfloat16):
    entries = jax.random.normal(rng, shape, jnp.float32) * spread
    if len(cuts) > 0:
        entries = block_levels(rng, shape, cuts, -0.22, 0.18) * entries
    return jnp.clip(entries, min=-most, max=most).astype(held_as)


def setup_inputs(seed: int = 0, part: int = 0) -> dict:
    arg_keys = jax.random.split(jax.random.key(seed), 11)
    part_keys = jax.random.split(jax.random.fold_in(arg_keys[10], part), 11)
    return {
        "prefill_blocks": draw_prefill_blocks(jax.random.fold_in(jax.random.fold_in(arg_keys[10], part), 71), part),
        "block_owner": draw_block_owner(jax.random.fold_in(jax.random.fold_in(arg_keys[10], part), 71), part),
        "block_position": draw_block_position(jax.random.fold_in(jax.random.fold_in(arg_keys[10], part), 71), part),
        "cache_len": draw_cache_len(jax.random.fold_in(jax.random.fold_in(arg_keys[10], part), 71), part),
        "query_nope": gaussian(part_keys[4], (REQUESTS, STEPS, HEADS, NOPE), 1.0, 6.0, ((2, 16),)),
        "query_rope": draw_query_rope(jax.random.fold_in(jax.random.fold_in(arg_keys[10], part), 71), part),
        "w_uk": gaussian(arg_keys[6], (HEADS, NOPE, KVL), NOPE ** -0.5, 0.5, ((0, 16),)),
        "w_uv": gaussian(arg_keys[7], (HEADS, KVL, VD), (KVL // 64) ** -0.5, 2.0, ((0, 16),)),
        "w_o": gaussian(arg_keys[8], (HEADS * VD, D), (HEADS * VD) ** -0.5, 0.046875, ((0, 16),)),
        "new_latent": gaussian(part_keys[9], (REQUESTS, STEPS, KVL + ROPE), 1.0, 6.0, ((0, 16),)),
    }


def reference(prefill_blocks, block_owner, block_position, cache_len, query_nope, query_rope, w_uk, w_uv, w_o, new_latent):
    q_latent = jnp.einsum("rshn,hnc->rshc", query_nope.astype(jnp.float32), w_uk.astype(jnp.float32)).astype(jnp.bfloat16)
    query_full = jnp.concatenate([q_latent, query_rope], axis=-1)
    score_scale = (NOPE + ROPE) ** -0.5
    target = jnp.where(block_owner >= 0, block_owner, REQUESTS).astype(jnp.int32)
    table = jnp.zeros((REQUESTS + 1, PRE_BLK), jnp.int32).at[target, block_position.astype(jnp.int32)].set(jnp.arange(SLOTS, dtype=jnp.int32))
    present = jnp.zeros((REQUESTS + 1, PRE_BLK), jnp.int32).at[target, block_position.astype(jnp.int32)].set(1)
    offsets = jnp.arange(PRE_BLK * BLK, dtype=jnp.int32)
    causal = jnp.arange(STEPS)[:, None] >= jnp.arange(STEPS)[None, :]
    causal_rows = jnp.repeat(causal, HEADS, axis=0)

    def per_request(index):
        key_rows = prefill_blocks[table[index]].reshape(PRE_BLK * BLK, KVL + ROPE)
        is_valid = (jnp.repeat(present[index], BLK) > 0) & (offsets < cache_len[index])
        query_rows = query_full[index].reshape(STEPS * HEADS, KVL + ROPE)
        fresh_keys = new_latent[index]
        old_scores = jnp.dot(query_rows, key_rows.T, preferred_element_type=jnp.float32) * score_scale
        new_scores = jnp.dot(query_rows, fresh_keys.T, preferred_element_type=jnp.float32) * score_scale
        old_scores = jnp.where(is_valid[None, :], old_scores, -1e30)
        new_scores = jnp.where(causal_rows, new_scores, -1e30)
        row_max = jnp.maximum(jnp.max(old_scores, axis=1), jnp.max(new_scores, axis=1))
        old_weights = jnp.where(is_valid[None, :], jnp.exp(old_scores - row_max[:, None]), 0.0)
        new_weights = jnp.where(causal_rows, jnp.exp(new_scores - row_max[:, None]), 0.0)
        weight_total = jnp.sum(old_weights, axis=1) + jnp.sum(new_weights, axis=1)
        summed = jnp.dot(old_weights.astype(jnp.bfloat16), key_rows[:, :KVL], preferred_element_type=jnp.float32)
        summed = summed + jnp.dot(new_weights.astype(jnp.bfloat16), fresh_keys[:, :KVL], preferred_element_type=jnp.float32)
        latent_out = (summed / weight_total[:, None]).astype(jnp.bfloat16).reshape(STEPS, HEADS, KVL)
        values = jnp.einsum("shc,hcv->shv", latent_out.astype(jnp.float32), w_uv.astype(jnp.float32)).astype(jnp.bfloat16)
        return jnp.dot(values.reshape(STEPS, HEADS * VD), w_o, preferred_element_type=jnp.float32).astype(jnp.bfloat16)

    return lax.map(per_request, jnp.arange(REQUESTS, dtype=jnp.int32))
```

```python
import functools
import math

import jax
import jax.numpy as jnp
from jax import lax
from jax.experimental import pallas as pl
from jax.experimental.pallas import tpu as pltpu
from jax.sharding import PartitionSpec as P

MIB = 1024 * 1024
Z, Y, C = 4, 2, 2
LOW = -1e30


def place():
    me = lax.axis_index("wide")
    return me, me // (Y * C), (me // C) % Y, me % C


def at(z, y, c):
    return {"wide": (z * Y + y) * C + c}


def remote(src, dst, send, recv, device):
    return pltpu.make_async_remote_copy(
        src_ref=src,
        dst_ref=dst,
        send_sem=send,
        recv_sem=recv,
        device_id=device,
        device_id_type=pl.DeviceIdType.MESH,
    )


def greet(c, chip):
    barrier = pltpu.get_barrier_semaphore()
    others = [(lax.rem(chip + d, Z * Y)) * C + c for d in range(1, Z * Y)]
    others.append(chip * C + 1 - c)
    for other in others:
        pl.semaphore_signal(
            barrier, inc=1, device_id={"wide": other}, device_id_type=pl.DeviceIdType.MESH
        )
    pl.semaphore_wait(barrier, len(others))


def gather_kernel(
    q_own, blocks, meta, q_all, sib, metas,
    local_sem, send_up, send_dn, send_y, recv_up, recv_dn, recv_y,
    one_send, one_recv, meta_send, meta_recv,
):
    me, z, y, c = place()
    chip = me // C
    greet(c, chip)
    sibling = at(z, y, 1 - c)

    def row(zs, ys, cc):
        return (zs * Y + ys) * C + (c if cc == 0 else 1 - c)

    own_local = pltpu.make_async_copy(q_own.at[c], q_all.at[me], local_sem.at[0])
    own_local.start()
    to_sib = remote(q_own.at[1 - c], q_all.at[me], one_send.at[0], one_recv.at[0], sibling)
    to_sib.start()
    meta_local = pltpu.make_async_copy(meta, metas.at[chip], local_sem.at[1])
    meta_local.start()
    meta_copies = []
    for d in range(1, Z * Y):
        copy = remote(
            meta, metas.at[chip], meta_send.at[d], meta_recv.at[d],
            {"wide": lax.rem(chip + d, Z * Y) * C + c},
        )
        copy.start()
        meta_copies.append(copy)
    copy = remote(meta, metas.at[Z * Y], meta_send.at[0], meta_recv.at[0], sibling)
    copy.start()
    meta_copies.append(copy)

    def up(d, cc):
        r = row(z - d, y, cc)
        src = q_own.at[c] if d == 0 and cc == 0 else q_all.at[r]
        return remote(src, q_all.at[r], send_up.at[d, cc], recv_up.at[d, cc], at(z + 1, y, c))

    def dn(d, cc):
        r = row(z + d, y, cc)
        src = q_own.at[c] if d == 0 and cc == 0 else q_all.at[r]
        return remote(src, q_all.at[r], send_dn.at[d, cc], recv_dn.at[d, cc], at(z - 1, y, c))

    def across(zs, cc, own=False):
        r = row(zs, y, cc)
        src = q_own.at[c] if own and cc == 0 else q_all.at[r]
        return remote(src, q_all.at[r], send_y.at[zs, cc], recv_y.at[zs, cc], at(z, 1 - y, c))

    key_copy = remote(blocks, sib, one_send.at[1], one_recv.at[1], sibling)
    for cc in range(2):
        if cc == 1:
            to_sib.wait_recv()
        pl.when(z < Z - 1)(lambda: up(0, cc).start())
        pl.when(z > 0)(lambda: dn(0, cc).start())
        across(z, cc, True).start()
    key_copy.start()
    for d in range(1, Z):
        for cc in range(2):

            @pl.when(z - d >= 0)
            def _():
                r = row(z - d, y, cc)
                remote(
                    q_all.at[r], q_all.at[r], send_up.at[d - 1, cc], recv_up.at[d - 1, cc], sibling
                ).wait_recv()
                if d < Z - 1:
                    pl.when(z < Z - 1)(lambda: up(d, cc).start())
                across(z - d, cc).start()

            @pl.when(z + d < Z)
            def _():
                r = row(z + d, y, cc)
                remote(
                    q_all.at[r], q_all.at[r], send_dn.at[d - 1, cc], recv_dn.at[d - 1, cc], sibling
                ).wait_recv()
                if d < Z - 1:
                    pl.when(z > 0)(lambda: dn(d, cc).start())
                across(z + d, cc).start()

    for zs in range(Z):
        for cc in range(2):
            r = row(zs, 1 - y, cc)
            remote(
                q_all.at[r], q_all.at[r], send_y.at[zs, cc], recv_y.at[zs, cc], sibling
            ).wait_recv()
            across(zs, cc).wait_send()
    for d in range(Z - 1):
        for cc in range(2):
            pl.when((z - d >= 0) & (z < Z - 1))(lambda: up(d, cc).wait_send())
            pl.when((z + d < Z) & (z > 0))(lambda: dn(d, cc).wait_send())
    to_sib.wait_send()
    key_copy.wait()
    own_local.wait()
    meta_local.wait()
    for copy in meta_copies:
        copy.wait()


def attention_kernel(scale, steps, heads, table, limits, where, q_ref, *refs):
    mine, theirs = refs[:8], refs[8:16]
    fresh_ref, o_ref, m_ref, keys = refs[16:]
    step = pl.program_id(0)
    tok = mine[0].shape[1]
    groups = q_ref.shape[0]
    per = steps * heads
    rows = groups * per
    latent = o_ref.shape[2]
    q_pair = q_ref[...].astype(jnp.float32)
    keys[8 * tok :, :] = fresh_ref[...]
    outs, maxes = [], []
    lane = lax.broadcasted_iota(jnp.int32, (1, tok), 1)
    lane_all = lax.broadcasted_iota(jnp.int32, (rows, tok), 1)
    step_of = (lax.broadcasted_iota(jnp.int32, (rows, tok), 0) % per) // heads
    for u in range(2):
        k = step * 2 + u
        query = q_pair[:, u * per : (u + 1) * per].reshape(rows, -1).astype(jnp.bfloat16)
        for s in range(4):
            keys[s * tok : (s + 1) * tok, :] = mine[u * 4 + s][0]
            keys[(4 + s) * tok : (5 + s) * tok, :] = theirs[u * 4 + s][0]
        scores = (
            lax.dot_general(
                query, keys[...], (((1,), (1,)), ((), ())), preferred_element_type=jnp.float32
            )
            * scale
        )
        parts = []
        for s in range(8):
            live = lane < limits[s // 4, k, s % 4]
            parts.append(jnp.where(live, scores[:, s * tok : (s + 1) * tok], LOW))
        bound = jnp.where(k == where[0], step_of, -1)
        parts.append(jnp.where(lane_all <= bound, scores[:, 8 * tok :], LOW))
        masked = jnp.concatenate(parts, axis=1)
        top = jnp.maximum(jnp.max(masked, axis=1, keepdims=True), -1e29)
        weights = jnp.exp(masked - top)
        total = jnp.sum(weights, axis=1, keepdims=True)
        out = jnp.dot(
            weights.astype(jnp.bfloat16), keys[:, :latent], preferred_element_type=jnp.float32
        )
        outs.append(out.reshape(groups, per, latent))
        stat = jnp.where(lane_all == 0, top, total)
        maxes.append(stat.reshape(groups, per, tok))
    o_ref[...] = jnp.concatenate(outs, axis=1).astype(jnp.bfloat16)
    m_ref[...] = jnp.concatenate(maxes, axis=1)


def reduce_kernel(
    o_ref, stat_ref, out_ref,
    stats, square, scaled, y_in, acc, up_in, dn_in, up_out, dn_out, fin, sib_in,
    stat_send, stat_recv, send_y, recv_y, send_up, recv_up, send_dn, recv_dn, sib_send, sib_recv,
):
    me, z, y, c = place()
    chip = me // C
    greet(c, chip)
    chips = Z * Y
    stat_copies = []
    for d in range(1, chips):
        copy = remote(
            stat_ref, stats.at[d], stat_send.at[d], stat_recv.at[d],
            {"wide": lax.rem(chip + d, chips) * C + c},
        )
        copy.start()
        stat_copies.append(copy)
    groups = stat_ref.shape[1]
    width = o_ref.shape[1]
    square[...] = jnp.zeros_like(square)
    stats[0] = stat_ref[...]
    for copy in stat_copies:
        copy.wait_recv()
    top = stats[0, 0]
    for d in range(1, chips):
        top = jnp.maximum(top, stats[d, 0])
    total = jnp.zeros_like(top)
    for d in range(chips):
        total += stats[d, 1] * jnp.exp(stats[d, 0] - top)
    square[:groups, :width] = jnp.exp(stats[0, 0] - top) / total
    square_t = square[...].T

    f_all = square_t[:width, :groups]

    def scale_chunk(base):
        for cc in range(C):
            j = base + cc
            lanes = lax.broadcasted_iota(jnp.int32, f_all.shape, 1)
            factor = jnp.sum(jnp.where(lanes == j, f_all, 0.0), axis=1, keepdims=True)
            scaled[j] = (o_ref[j].astype(jnp.float32) * factor).astype(jnp.bfloat16)

    order = (3, 0, 2, 1)

    def y_copy(t):
        base = (t * Y + 1 - y) * C
        return remote(
            scaled.at[pl.ds(base, C)], y_in.at[t], send_y.at[t], recv_y.at[t], at(z, 1 - y, c)
        )

    for t in order:
        scale_chunk((t * Y + 1 - y) * C)
        y_copy(t).start()
    for t in order:
        scale_chunk((t * Y + y) * C)

    def up_copy(t):
        return remote(
            up_out.at[t], up_in.at[t], send_up.at[t], recv_up.at[t], at(z + 1, y, c)
        )

    def dn_copy(t):
        return remote(
            dn_out.at[t], dn_in.at[t], send_dn.at[t], recv_dn.at[t], at(z - 1, y, c)
        )

    def up_arrived(t):
        remote(
            up_out.at[t], up_in.at[t], send_up.at[t], recv_up.at[t], at(z, y, 1 - c)
        ).wait_recv()

    def dn_arrived(t):
        remote(
            dn_out.at[t], dn_in.at[t], send_dn.at[t], recv_dn.at[t], at(z, y, 1 - c)
        ).wait_recv()

    def get_y(t):
        y_copy(t).wait_recv()
        mine = scaled[pl.ds((t * Y + y) * C, C)].astype(jnp.float32)
        acc[t] = mine + y_in[t].astype(jnp.float32)

    def send_upward(t):
        @pl.when(z == 0)
        def _():
            up_out[t] = acc[t].astype(jnp.bfloat16)

        @pl.when((z > 0) & (z < t))
        def _():
            up_arrived(t)
            up_out[t] = (acc[t] + up_in[t].astype(jnp.float32)).astype(jnp.bfloat16)

        pl.when(z < t)(lambda: up_copy(t).start())

    def send_downward(t):
        @pl.when(z == Z - 1)
        def _():
            dn_out[t] = acc[t].astype(jnp.bfloat16)

        @pl.when((z < Z - 1) & (z > t))
        def _():
            dn_arrived(t)
            dn_out[t] = (acc[t] + dn_in[t].astype(jnp.float32)).astype(jnp.bfloat16)

        pl.when(z > t)(lambda: dn_copy(t).start())

    get_y(3)
    send_upward(3)
    get_y(0)
    send_downward(0)
    get_y(2)
    send_upward(2)
    get_y(1)
    send_downward(1)
    send_upward(1)
    send_downward(2)
    for t in range(Z):

        @pl.when(z == t)
        def _():
            value = acc[t]
            if t > 0:
                up_arrived(t)
                value = value + up_in[t].astype(jnp.float32)
            if t < Z - 1:
                dn_arrived(t)
                value = value + dn_in[t].astype(jnp.float32)
            fin[...] = value.astype(jnp.bfloat16)

    swap = remote(fin.at[1 - c], sib_in, sib_send, sib_recv, at(z, y, 1 - c))
    swap.start()
    out_ref[c] = fin[c]
    swap.wait()
    out_ref[1 - c] = sib_in[...]
    for t in range(Z):
        y_copy(t).wait_send()
        pl.when(z < t)(lambda: up_copy(t).wait_send())
        pl.when(z > t)(lambda: dn_copy(t).wait_send())
    for copy in stat_copies:
        copy.wait_send()


def move_queries(
    prefill_blocks, block_owner, block_position, cache_len,
    query_nope, query_rope, w_uk, w_uv, w_o, new_latent,
):
    members = lax.axis_size("wide")
    slots, tok, width = prefill_blocks.shape
    latent = w_uk.shape[2]
    requests, steps, heads = query_nope.shape[:3]
    per = steps * heads
    half = members // C
    rows = half * per
    per_peer = (slots + members - 1) // members
    me, z, y, c = place()
    chip = me // C
    scale = (query_nope.shape[3] + query_rope.shape[3]) ** (-0.5)

    order = jnp.arange(slots)
    same = (block_owner[:, None] == block_owner[None, :]) & (order[None, :] < order[:, None])
    rank = jnp.sum(same.astype(jnp.int32), axis=1)
    slot_of = jnp.where(block_owner >= 0, block_owner * per_peer + rank, members * per_peer)
    matches = slot_of[None, :] == jnp.arange(members * per_peer)[:, None]
    source = jnp.sum(jnp.where(matches, order[None, :], 0), axis=1)
    place_of = jnp.sum(jnp.where(matches, block_position[None, :] + 1, 0), axis=1)
    channels = members * per_peer
    meta = jnp.concatenate(
        [
            jnp.concatenate([source, place_of])[None, :],
            jnp.broadcast_to(cache_len[:1, None], (7, 2 * channels)),
        ]
    ).astype(jnp.int32)

    q_latent = jnp.einsum(
        "rshn,hnc->rshc", query_nope, w_uk, preferred_element_type=jnp.float32
    ).astype(jnp.bfloat16)
    q_full = jnp.concatenate([q_latent, query_rope], axis=3)
    q_own = q_full.reshape(half, C, per, width).transpose(1, 0, 2, 3).reshape(C, rows, width)

    anywhere = pl.BlockSpec(memory_space=pl.ANY)
    vmem = pl.BlockSpec(memory_space=pltpu.VMEM)
    dma = pltpu.SemaphoreType.DMA
    q_all, sib, metas = pl.pallas_call(
        gather_kernel,
        out_shape=(
            jax.ShapeDtypeStruct((members, rows, width), jnp.bfloat16),
            jax.ShapeDtypeStruct(prefill_blocks.shape, jnp.bfloat16),
            jax.ShapeDtypeStruct((half + 1,) + meta.shape, jnp.int32),
        ),
        in_specs=[anywhere] * 3,
        out_specs=(anywhere,) * 3,
        scratch_shapes=[
            dma((2,)),
            dma((Z, 2)), dma((Z, 2)), dma((Z, 2)),
            dma((Z, 2)), dma((Z, 2)), dma((Z, 2)),
            dma((2,)), dma((2,)), dma((half,)), dma((half,)),
        ],
        compiler_params=pltpu.CompilerParams(collective_id=0, has_side_effects=True),
        name="gather_queries",
    )(q_own, prefill_blocks, meta)

    def my_side(tag_row):
        both = tag_row[0].reshape(2, half, C, per_peer)
        return jnp.where(c == 0, both[:, :, 0], both[:, :, 1])

    mine, theirs = my_side(meta), my_side(metas[half])
    table = jnp.stack([mine[0], theirs[0]])
    spots = jnp.stack([mine[1], theirs[1]])
    lengths = metas[:half, 1, 0]
    limits = jnp.where(spots > 0, lengths[None, :, None] - (spots - 1) * tok, 0)
    fresh = jnp.zeros((tok, width), jnp.bfloat16).at[:steps].set(new_latent[0])

    def key_spec(side, u, s):
        return pl.BlockSpec(
            (1, tok, width), lambda g, table, limits, where: (table[side, 2 * g + u, s], 0, 0)
        )

    pairs = [(u, s) for u in range(2) for s in range(per_peer)]
    partial, stat = pl.pallas_call(
        functools.partial(attention_kernel, scale, steps, heads),
        out_shape=(
            jax.ShapeDtypeStruct((members, rows, latent), jnp.bfloat16),
            jax.ShapeDtypeStruct((members, rows, tok), jnp.float32),
        ),
        grid_spec=pltpu.PrefetchScalarGridSpec(
            num_scalar_prefetch=3,
            grid=(half // 2,),
            in_specs=[pl.BlockSpec((members, 2 * per, width), lambda g, *_: (0, g, 0))]
            + [key_spec(0, u, s) for u, s in pairs]
            + [key_spec(1, u, s) for u, s in pairs]
            + [pl.BlockSpec((tok, width), lambda g, *_: (0, 0))],
            out_specs=(
                pl.BlockSpec((members, 2 * per, latent), lambda g, *_: (0, g, 0)),
                pl.BlockSpec((members, 2 * per, tok), lambda g, *_: (0, g, 0)),
            ),
            scratch_shapes=[pltpu.VMEM(((2 * per_peer + 1) * tok, width), jnp.bfloat16)],
        ),
        compiler_params=pltpu.CompilerParams(vmem_limit_bytes=48 * MIB),
        name="partial_attention",
    )(
        table, limits, chip.reshape(1), q_all,
        *([prefill_blocks] * len(pairs)), *([sib] * len(pairs)), fresh,
    )
    stat_rows = stat[:, :, :2].transpose(2, 0, 1)

    chunk = (C, rows, latent)
    gathered = pl.pallas_call(
        reduce_kernel,
        out_shape=jax.ShapeDtypeStruct((C, rows, latent), jnp.bfloat16),
        in_specs=[vmem, vmem],
        out_specs=vmem,
        scratch_shapes=[
            pltpu.VMEM((half, 2, members, rows), jnp.float32),
            pltpu.VMEM((128, 256), jnp.float32),
            pltpu.VMEM((members, rows, latent), jnp.bfloat16),
            pltpu.VMEM((Z,) + chunk, jnp.bfloat16),
            pltpu.VMEM((Z,) + chunk, jnp.float32),
            pltpu.VMEM((Z,) + chunk, jnp.bfloat16),
            pltpu.VMEM((Z,) + chunk, jnp.bfloat16),
            pltpu.VMEM((Z,) + chunk, jnp.bfloat16),
            pltpu.VMEM((Z,) + chunk, jnp.bfloat16),
            pltpu.VMEM(chunk, jnp.bfloat16),
            pltpu.VMEM(chunk[1:], jnp.bfloat16),
            dma((half,)), dma((half,)),
            dma((Z,)), dma((Z,)), dma((Z,)), dma((Z,)), dma((Z,)), dma((Z,)),
            dma, dma,
        ],
        compiler_params=pltpu.CompilerParams(
            collective_id=1, has_side_effects=True, vmem_limit_bytes=48 * MIB
        ),
        name="reduce_partials",
    )(partial, stat_rows)

    latents = gathered.reshape(C, half, steps, heads, latent)
    values = jnp.einsum(
        "pkshc,hcv->kpshv", latents, w_uv, preferred_element_type=jnp.float32
    ).astype(jnp.bfloat16)
    values = values.reshape(members * steps, -1)
    share = jnp.dot(values, w_o, preferred_element_type=jnp.float32).astype(jnp.bfloat16)
    share = share.reshape(members, steps, -1)
    shares = lax.all_to_all(share, "wide", split_axis=0, concat_axis=0, tiled=True)
    return jnp.sum(shares.astype(jnp.float32), axis=0, keepdims=True).astype(jnp.bfloat16)


def move_keys(
    prefill_blocks,
    block_owner,
    block_position,
    cache_len,
    query_nope,
    query_rope,
    w_uk,
    w_uv,
    w_o,
    new_latent,
):
    members = lax.axis_size("wide")
    local_slots = prefill_blocks.shape[0]
    block_tok = prefill_blocks.shape[1]
    key_width = prefill_blocks.shape[2]
    latent = w_uk.shape[2]
    per_peer = (local_slots + members - 1) // members
    channels = members * per_peer
    is_live = block_owner >= 0
    target = jnp.where(is_live, block_owner, members)
    slot_order = jnp.arange(local_slots)
    same_peer = (target[:, None] == target[None, :]) & (slot_order[None, :] < slot_order[:, None])
    peer_rank = jnp.sum(same_peer.astype(jnp.int32), axis=1)
    slot_of = jnp.where(is_live, target * per_peer + peer_rank, channels)
    matches = slot_of[None, :] == jnp.arange(channels)[:, None]
    source_row = jnp.sum(jnp.where(matches, slot_order[None, :], 0), axis=1)
    filled = jnp.any(matches, axis=1)
    outgoing = jnp.where(
        filled[:, None, None], prefill_blocks[source_row], jnp.zeros((), prefill_blocks.dtype)
    )
    tag_values = jnp.where(filled, block_position[source_row] + 1, 0).astype(jnp.bfloat16)
    q_latent = jnp.einsum(
        "rshn,hnc->rshc", query_nope, w_uk, preferred_element_type=jnp.float32
    ).astype(jnp.bfloat16)
    query_full = jnp.concatenate([q_latent, query_rope], axis=3)
    step_count = query_full.shape[1]
    heads_here = query_full.shape[2]
    heads_all = members * heads_here
    incoming, arrived = (
        lax.all_to_all(outgoing, "wide", split_axis=0, concat_axis=0, tiled=True),
        lax.all_to_all(tag_values, "wide", split_axis=0, concat_axis=0, tiled=True),
    )
    gathered = lax.all_to_all(query_full, "wide", split_axis=0, concat_axis=2, tiled=True)
    query_rows = gathered.reshape(step_count * heads_all, key_width)
    my_len = cache_len[0]
    position = arrived.astype(jnp.int32)
    tokens = jnp.arange(block_tok)
    is_valid = (position[:, None] > 0) & (
        (position[:, None] - 1) * block_tok + tokens[None, :] < my_len
    )
    score_scale = (query_nope.shape[3] + query_rope.shape[3]) ** (-0.5)
    flat_keys = incoming.reshape(-1, key_width)
    flat_valid = is_valid.reshape(-1)
    block_rows = math.gcd(flat_keys.shape[0], 1024)
    key_blocks = flat_keys.reshape(-1, block_rows, key_width)
    valid_blocks = flat_valid.reshape(-1, block_rows)
    total_rows = query_rows.shape[0]

    def absorb(carry, key_rows, key_mask):
        running_max, weight_total, summed = carry
        scores = (
            lax.dot_general(
                query_rows, key_rows, (((1,), (1,)), ((), ())), preferred_element_type=jnp.float32
            )
            * score_scale
        )
        scores = jnp.where(key_mask, scores, -1e30)
        fresh_max = jnp.maximum(running_max, jnp.max(scores, axis=1))
        weights = jnp.where(key_mask, jnp.exp(scores - fresh_max[:, None]), 0.0)
        factor = jnp.exp(running_max - fresh_max)
        weight_total = weight_total * factor + jnp.sum(weights, axis=1)
        summed = summed * factor[:, None] + jnp.dot(
            weights.astype(jnp.bfloat16), key_rows[:, :latent], preferred_element_type=jnp.float32
        )
        return (fresh_max, weight_total, summed)

    def scan_step(carry, inputs):
        return (absorb(carry, inputs[0], inputs[1][None, :]), None)

    start_state = (
        jnp.full((total_rows,), -1e30, jnp.float32),
        jnp.zeros((total_rows,), jnp.float32),
        jnp.zeros((total_rows, latent), jnp.float32),
    )
    state, _ = lax.scan(scan_step, start_state, (key_blocks, valid_blocks))
    fresh_keys = new_latent[0]
    causal_mask = (jnp.arange(total_rows) // heads_all)[:, None] >= jnp.arange(step_count)[None, :]
    running_max, weight_total, summed = absorb(state, fresh_keys, causal_mask)
    latent_out = (
        (summed / weight_total[:, None])
        .astype(jnp.bfloat16)
        .reshape(1, step_count, heads_all, latent)
    )
    returned = lax.all_to_all(latent_out, "wide", split_axis=2, concat_axis=0, tiled=True)
    values = jnp.einsum(
        "rshc,hcv->rshv", returned, w_uv, preferred_element_type=jnp.float32
    ).astype(jnp.bfloat16)
    values = values.reshape(members, step_count, -1)
    layer_out = lax.psum_scatter(
        jnp.einsum("rsk,kd->rsd", values, w_o, preferred_element_type=jnp.float32),
        "wide",
        scatter_dimension=0,
        tiled=True,
    )
    return layer_out.astype(jnp.bfloat16)


def solution(mesh):
    in_specs = (
        P(("groups", "wide"), None, None),
        P(("groups", "wide")),
        P(("groups", "wide")),
        P(("groups", "wide")),
        P("groups", None, "wide", None),
        P("groups", None, "wide", None),
        P("wide", None, None),
        P("wide", None, None),
        P("wide", None),
        P(("groups", "wide"), None, None),
    )
    per_device = move_queries if mesh.shape["wide"] == Z * Y * C else move_keys
    out_specs = P(("groups", "wide"), None, None)
    return jax.shard_map(
        per_device, mesh=mesh, in_specs=in_specs, out_specs=out_specs, check_vma=False
    )
```

```python
import functools
import math

import jax
import jax.numpy as jnp
from jax import lax
from jax.experimental import pallas as pl
from jax.experimental.pallas import tpu as pltpu
from jax.sharding import PartitionSpec as P

MIB = 1024 * 1024
Z, Y, C = 4, 2, 2
LOW = -1e30


def place():
    me = lax.axis_index("wide")
    return me, me // (Y * C), (me // C) % Y, me % C


def at(z, y, c):
    return {"wide": (z * Y + y) * C + c}


def remote(src, dst, send, recv, device):
    return pltpu.make_async_remote_copy(
        src_ref=src,
        dst_ref=dst,
        send_sem=send,
        recv_sem=recv,
        device_id=device,
        device_id_type=pl.DeviceIdType.MESH,
    )


def greet(c, chip):
    barrier = pltpu.get_barrier_semaphore()
    others = [(lax.rem(chip + d, Z * Y)) * C + c for d in range(1, Z * Y)]
    others.append(chip * C + 1 - c)
    for other in others:
        pl.semaphore_signal(
            barrier, inc=1, device_id={"wide": other}, device_id_type=pl.DeviceIdType.MESH
        )
    pl.semaphore_wait(barrier, len(others))


def gather_kernel(
    q_own, blocks, meta, q_all, sib, metas,
    local_sem, send_up, send_dn, send_y, recv_up, recv_dn, recv_y,
    one_send, one_recv, meta_send, meta_recv,
):
    me, z, y, c = place()
    chip = me // C
    greet(c, chip)
    sibling = at(z, y, 1 - c)

    def row(zs, ys, cc):
        return (zs * Y + ys) * C + (c if cc == 0 else 1 - c)

    own_local = pltpu.make_async_copy(q_own.at[c], q_all.at[me], local_sem.at[0])
    own_local.start()
    to_sib = remote(q_own.at[1 - c], q_all.at[me], one_send.at[0], one_recv.at[0], sibling)
    to_sib.start()
    meta_local = pltpu.make_async_copy(meta, metas.at[chip], local_sem.at[1])
    meta_local.start()
    meta_copies = []
    for d in range(1, Z * Y):
        copy = remote(
            meta, metas.at[chip], meta_send.at[d], meta_recv.at[d],
            {"wide": lax.rem(chip + d, Z * Y) * C + c},
        )
        copy.start()
        meta_copies.append(copy)
    copy = remote(meta, metas.at[Z * Y], meta_send.at[0], meta_recv.at[0], sibling)
    copy.start()
    meta_copies.append(copy)

    def up(d, cc):
        r = row(z - d, y, cc)
        src = q_own.at[c] if d == 0 and cc == 0 else q_all.at[r]
        return remote(src, q_all.at[r], send_up.at[d, cc], recv_up.at[d, cc], at(z + 1, y, c))

    def dn(d, cc):
        r = row(z + d, y, cc)
        src = q_own.at[c] if d == 0 and cc == 0 else q_all.at[r]
        return remote(src, q_all.at[r], send_dn.at[d, cc], recv_dn.at[d, cc], at(z - 1, y, c))

    def across(zs, cc, own=False):
        r = row(zs, y, cc)
        src = q_own.at[c] if own and cc == 0 else q_all.at[r]
        return remote(src, q_all.at[r], send_y.at[zs, cc], recv_y.at[zs, cc], at(z, 1 - y, c))

    key_copy = remote(blocks, sib, one_send.at[1], one_recv.at[1], sibling)
    for cc in range(2):
        if cc == 1:
            to_sib.wait_recv()
        pl.when(z < Z - 1)(lambda: up(0, cc).start())
        pl.when(z > 0)(lambda: dn(0, cc).start())
        across(z, cc, True).start()
    key_copy.start()
    for d in range(1, Z):
        for cc in range(2):

            @pl.when(z - d >= 0)
            def _():
                r = row(z - d, y, cc)
                remote(
                    q_all.at[r], q_all.at[r], send_up.at[d - 1, cc], recv_up.at[d - 1, cc], sibling
                ).wait_recv()
                if d < Z - 1:
                    pl.when(z < Z - 1)(lambda: up(d, cc).start())
                across(z - d, cc).start()

            @pl.when(z + d < Z)
            def _():
                r = row(z + d, y, cc)
                remote(
                    q_all.at[r], q_all.at[r], send_dn.at[d - 1, cc], recv_dn.at[d - 1, cc], sibling
                ).wait_recv()
                if d < Z - 1:
                    pl.when(z > 0)(lambda: dn(d, cc).start())
                across(z + d, cc).start()

    for zs in range(Z):
        for cc in range(2):
            r = row(zs, 1 - y, cc)
            remote(
                q_all.at[r], q_all.at[r], send_y.at[zs, cc], recv_y.at[zs, cc], sibling
            ).wait_recv()
            across(zs, cc).wait_send()
    for d in range(Z - 1):
        for cc in range(2):
            pl.when((z - d >= 0) & (z < Z - 1))(lambda: up(d, cc).wait_send())
            pl.when((z + d < Z) & (z > 0))(lambda: dn(d, cc).wait_send())
    to_sib.wait_send()
    key_copy.wait()
    own_local.wait()
    meta_local.wait()
    for copy in meta_copies:
        copy.wait()


def attention_kernel(scale, steps, heads, table, limits, where, q_ref, *refs):
    mine, theirs = refs[:8], refs[8:16]
    fresh_ref, o_ref, m_ref, keys = refs[16:]
    step = pl.program_id(0)
    tok = mine[0].shape[2]
    groups = q_ref.shape[0]
    per = steps * heads
    rows = groups * per
    latent = o_ref.shape[2]
    q_pair = q_ref[...].astype(jnp.float32)
    keys[:, 8 * tok :] = fresh_ref[...]
    outs, maxes = [], []
    lane = lax.broadcasted_iota(jnp.int32, (1, tok), 1)
    lane_all = lax.broadcasted_iota(jnp.int32, (rows, tok), 1)
    step_of = (lax.broadcasted_iota(jnp.int32, (rows, tok), 0) % per) // heads
    for u in range(2):
        k = step * 2 + u
        query = q_pair[:, u * per : (u + 1) * per].reshape(rows, -1).astype(jnp.bfloat16)
        for s in range(4):
            keys[:, s * tok : (s + 1) * tok] = mine[u * 4 + s][0]
            keys[:, (4 + s) * tok : (5 + s) * tok] = theirs[u * 4 + s][0]
        scores = (
            jnp.dot(query, keys[...], preferred_element_type=jnp.float32)
            * scale
        )
        parts = []
        for s in range(8):
            live = lane < limits[s // 4, k, s % 4]
            parts.append(jnp.where(live, scores[:, s * tok : (s + 1) * tok], LOW))
        bound = jnp.where(k == where[0], step_of, -1)
        parts.append(jnp.where(lane_all <= bound, scores[:, 8 * tok :], LOW))
        masked = jnp.concatenate(parts, axis=1)
        top = jnp.maximum(jnp.max(masked, axis=1, keepdims=True), -1e29)
        weights = jnp.exp(masked - top)
        total = jnp.sum(weights, axis=1, keepdims=True)
        out = lax.dot_general(
            weights.astype(jnp.bfloat16),
            keys[:latent, :],
            (((1,), (1,)), ((), ())),
            preferred_element_type=jnp.float32,
        )
        outs.append(out.reshape(groups, per, latent))
        stat = jnp.where(lane_all == 0, top, total)
        maxes.append(stat.reshape(groups, per, tok))
    o_ref[...] = jnp.concatenate(outs, axis=1).astype(jnp.bfloat16)
    m_ref[...] = jnp.concatenate(maxes, axis=1)


def reduce_kernel(
    steps, heads, o_ref, stat_ref, w_uv_ref, w_o_ref, out_ref,
    stats, square, scaled, y_in, acc, up_in, dn_in, up_out, dn_out, fin, sib_in,
    w_o, part, part_in, rows_f, message, inbox,
    stat_send, stat_recv, send_y, recv_y, send_up, recv_up, send_dn, recv_dn, sib_send, sib_recv,
    load_sem, part_send, part_recv, row_send, row_recv,
):
    me, z, y, c = place()
    chip = me // C
    greet(c, chip)
    chips = Z * Y
    stat_copies = []
    for d in range(1, chips):
        copy = remote(
            stat_ref, stats.at[d], stat_send.at[d], stat_recv.at[d],
            {"wide": lax.rem(chip + d, chips) * C + c},
        )
        copy.start()
        stat_copies.append(copy)
    load = pltpu.make_async_copy(w_o_ref, w_o, load_sem)
    load.start()
    groups = stat_ref.shape[1]
    width = o_ref.shape[1]
    square[...] = jnp.zeros_like(square)
    stats[0] = stat_ref[...]
    for copy in stat_copies:
        copy.wait_recv()
    top = stats[0, 0]
    for d in range(1, chips):
        top = jnp.maximum(top, stats[d, 0])
    total = jnp.zeros_like(top)
    for d in range(chips):
        total += stats[d, 1] * jnp.exp(stats[d, 0] - top)
    square[:groups, :width] = jnp.exp(stats[0, 0] - top) / total
    square_t = square[...].T

    f_all = square_t[:width, :groups]

    def scale_chunk(base):
        for cc in range(C):
            j = base + cc
            lanes = lax.broadcasted_iota(jnp.int32, f_all.shape, 1)
            factor = jnp.sum(jnp.where(lanes == j, f_all, 0.0), axis=1, keepdims=True)
            scaled[j] = (o_ref[j].astype(jnp.float32) * factor).astype(jnp.bfloat16)

    order = (3, 0, 2, 1)

    def y_copy(t):
        base = (t * Y + 1 - y) * C
        return remote(
            scaled.at[pl.ds(base, C)], y_in.at[t], send_y.at[t], recv_y.at[t], at(z, 1 - y, c)
        )

    for t in order:
        scale_chunk((t * Y + 1 - y) * C)
        y_copy(t).start()
    for t in order:
        scale_chunk((t * Y + y) * C)

    def up_copy(t):
        return remote(
            up_out.at[t], up_in.at[t], send_up.at[t], recv_up.at[t], at(z + 1, y, c)
        )

    def dn_copy(t):
        return remote(
            dn_out.at[t], dn_in.at[t], send_dn.at[t], recv_dn.at[t], at(z - 1, y, c)
        )

    def up_arrived(t):
        remote(
            up_out.at[t], up_in.at[t], send_up.at[t], recv_up.at[t], at(z, y, 1 - c)
        ).wait_recv()

    def dn_arrived(t):
        remote(
            dn_out.at[t], dn_in.at[t], send_dn.at[t], recv_dn.at[t], at(z, y, 1 - c)
        ).wait_recv()

    def get_y(t):
        y_copy(t).wait_recv()
        mine = scaled[pl.ds((t * Y + y) * C, C)].astype(jnp.float32)
        acc[t] = mine + y_in[t].astype(jnp.float32)

    def send_upward(t):
        @pl.when(z == 0)
        def _():
            up_out[t] = acc[t].astype(jnp.bfloat16)

        @pl.when((z > 0) & (z < t))
        def _():
            up_arrived(t)
            up_out[t] = (acc[t] + up_in[t].astype(jnp.float32)).astype(jnp.bfloat16)

        pl.when(z < t)(lambda: up_copy(t).start())

    def send_downward(t):
        @pl.when(z == Z - 1)
        def _():
            dn_out[t] = acc[t].astype(jnp.bfloat16)

        @pl.when((z < Z - 1) & (z > t))
        def _():
            dn_arrived(t)
            dn_out[t] = (acc[t] + dn_in[t].astype(jnp.float32)).astype(jnp.bfloat16)

        pl.when(z > t)(lambda: dn_copy(t).start())

    get_y(3)
    send_upward(3)
    get_y(0)
    send_downward(0)
    get_y(2)
    send_upward(2)
    get_y(1)
    send_downward(1)
    send_upward(1)
    send_downward(2)
    for t in range(Z):

        @pl.when(z == t)
        def _():
            value = acc[t]
            if t > 0:
                up_arrived(t)
                value = value + up_in[t].astype(jnp.float32)
            if t < Z - 1:
                dn_arrived(t)
                value = value + dn_in[t].astype(jnp.float32)
            fin[...] = value.astype(jnp.bfloat16)

    swap = remote(fin.at[1 - c], sib_in, sib_send, sib_recv, at(z, y, 1 - c))
    swap.start()
    per = chips * steps
    swap.wait()
    even = jnp.where(c == 0, fin[c], sib_in[...])
    odd = jnp.where(c == 0, sib_in[...], fin[c])
    both = jnp.concatenate([even, odd], axis=0)
    row_head = lax.broadcasted_iota(jnp.int32, (both.shape[0], w_uv_ref.shape[2]), 0) % heads
    values = []
    for h in range(heads):
        every = jnp.dot(both, w_uv_ref[h], preferred_element_type=jnp.float32)
        every = jnp.where(row_head == h, every, 0.0)
        values.append(jnp.sum(every.reshape(C * per, heads, -1), axis=1))
    values = jnp.concatenate(values, axis=1).astype(jnp.bfloat16)
    rows_f[...] = jnp.zeros_like(rows_f)
    load.wait()
    tiles, _, wide = part_in.shape

    def part_copy(i):
        return remote(
            part.at[1 - c, i], part_in.at[i], part_send.at[i], part_recv.at[i], at(z, y, 1 - c)
        )

    for i in range(tiles):
        share = jnp.dot(
            values, w_o[:, i * wide : (i + 1) * wide], preferred_element_type=jnp.float32
        )
        part[0, i] = share[:per]
        part[1, i] = share[per:]
        part_copy(i).start()
    for i in range(tiles):
        part_copy(i).wait_recv()
        summed = part[c, i] + part_in[i]
        for k in range(chips):
            rows_f[k, i * steps : (i + 1) * steps, :] = summed[k * steps : (k + 1) * steps]
    message[...] = rows_f[...].astype(jnp.bfloat16)
    row_copies = []
    for d in range(1, chips):
        other = lax.rem(chip + d, chips)
        copy = remote(
            message.at[other], inbox.at[d - 1], row_send.at[d - 1], row_recv.at[d - 1],
            {"wide": other * C + c},
        )
        copy.start()
        row_copies.append(copy)
    result = rows_f[chip]
    for d in range(1, chips):
        row_copies[d - 1].wait_recv()
        result = result + inbox[d - 1].astype(jnp.float32)
    out_ref[...] = result.astype(jnp.bfloat16)
    for i in range(tiles):
        part_copy(i).wait_send()
    for copy in row_copies:
        copy.wait_send()
    for t in range(Z):
        y_copy(t).wait_send()
        pl.when(z < t)(lambda: up_copy(t).wait_send())
        pl.when(z > t)(lambda: dn_copy(t).wait_send())
    for copy in stat_copies:
        copy.wait_send()


def move_queries(
    prefill_blocks, block_owner, block_position, cache_len,
    query_nope, query_rope, w_uk, w_uv, w_o, new_latent,
):
    members = lax.axis_size("wide")
    slots, tok, width = prefill_blocks.shape
    latent = w_uk.shape[2]
    requests, steps, heads = query_nope.shape[:3]
    per = steps * heads
    half = members // C
    rows = half * per
    per_peer = (slots + members - 1) // members
    blocks_t = jnp.swapaxes(prefill_blocks, 1, 2)
    me, z, y, c = place()
    chip = me // C
    scale = (query_nope.shape[3] + query_rope.shape[3]) ** (-0.5)

    order = jnp.arange(slots)
    same = (block_owner[:, None] == block_owner[None, :]) & (order[None, :] < order[:, None])
    rank = jnp.sum(same.astype(jnp.int32), axis=1)
    slot_of = jnp.where(block_owner >= 0, block_owner * per_peer + rank, members * per_peer)
    matches = slot_of[None, :] == jnp.arange(members * per_peer)[:, None]
    source = jnp.sum(jnp.where(matches, order[None, :], 0), axis=1)
    place_of = jnp.sum(jnp.where(matches, block_position[None, :] + 1, 0), axis=1)
    channels = members * per_peer
    meta = jnp.concatenate(
        [
            jnp.concatenate([source, place_of])[None, :],
            jnp.broadcast_to(cache_len[:1, None], (7, 2 * channels)),
        ]
    ).astype(jnp.int32)

    q_latent = jnp.einsum(
        "rshn,hnc->rshc", query_nope, w_uk, preferred_element_type=jnp.float32
    ).astype(jnp.bfloat16)
    q_full = jnp.concatenate([q_latent, query_rope], axis=3)
    q_own = q_full.reshape(half, C, per, width).transpose(1, 0, 2, 3).reshape(C, rows, width)

    anywhere = pl.BlockSpec(memory_space=pl.ANY)
    vmem = pl.BlockSpec(memory_space=pltpu.VMEM)
    dma = pltpu.SemaphoreType.DMA
    q_all, sib, metas = pl.pallas_call(
        gather_kernel,
        out_shape=(
            jax.ShapeDtypeStruct((members, rows, width), jnp.bfloat16),
            jax.ShapeDtypeStruct(blocks_t.shape, jnp.bfloat16),
            jax.ShapeDtypeStruct((half + 1,) + meta.shape, jnp.int32),
        ),
        in_specs=[anywhere] * 3,
        out_specs=(anywhere,) * 3,
        scratch_shapes=[
            dma((2,)),
            dma((Z, 2)), dma((Z, 2)), dma((Z, 2)),
            dma((Z, 2)), dma((Z, 2)), dma((Z, 2)),
            dma((2,)), dma((2,)), dma((half,)), dma((half,)),
        ],
        compiler_params=pltpu.CompilerParams(collective_id=0, has_side_effects=True),
        name="gather_queries",
    )(q_own, blocks_t, meta)

    def my_side(tag_row):
        both = tag_row[0].reshape(2, half, C, per_peer)
        return jnp.where(c == 0, both[:, :, 0], both[:, :, 1])

    mine, theirs = my_side(meta), my_side(metas[half])
    table = jnp.stack([mine[0], theirs[0]])
    spots = jnp.stack([mine[1], theirs[1]])
    lengths = metas[:half, 1, 0]
    limits = jnp.where(spots > 0, lengths[None, :, None] - (spots - 1) * tok, 0)
    fresh = jnp.zeros((width, tok), jnp.bfloat16).at[:, :steps].set(new_latent[0].T)

    def key_spec(side, u, s):
        return pl.BlockSpec(
            (1, width, tok), lambda g, table, limits, where: (table[side, 2 * g + u, s], 0, 0)
        )

    pairs = [(u, s) for u in range(2) for s in range(per_peer)]
    partial, stat = pl.pallas_call(
        functools.partial(attention_kernel, scale, steps, heads),
        out_shape=(
            jax.ShapeDtypeStruct((members, rows, latent), jnp.bfloat16),
            jax.ShapeDtypeStruct((members, rows, tok), jnp.float32),
        ),
        grid_spec=pltpu.PrefetchScalarGridSpec(
            num_scalar_prefetch=3,
            grid=(half // 2,),
            in_specs=[pl.BlockSpec((members, 2 * per, width), lambda g, *_: (0, g, 0))]
            + [key_spec(0, u, s) for u, s in pairs]
            + [key_spec(1, u, s) for u, s in pairs]
            + [pl.BlockSpec((width, tok), lambda g, *_: (0, 0))],
            out_specs=(
                pl.BlockSpec((members, 2 * per, latent), lambda g, *_: (0, g, 0)),
                pl.BlockSpec((members, 2 * per, tok), lambda g, *_: (0, g, 0)),
            ),
            scratch_shapes=[pltpu.VMEM((width, (2 * per_peer + 1) * tok), jnp.bfloat16)],
        ),
        compiler_params=pltpu.CompilerParams(vmem_limit_bytes=48 * MIB),
        name="partial_attention",
    )(
        table, limits, chip.reshape(1), q_all,
        *([blocks_t] * len(pairs)), *([sib] * len(pairs)), fresh,
    )
    stat_rows = stat[:, :, :2].transpose(2, 0, 1)

    chunk = (C, rows, latent)
    model = w_o.shape[1]
    tile = math.gcd(model, 512)
    tiles = model // tile
    tall = (tiles * steps + 15) // 16 * 16
    out = pl.pallas_call(
        functools.partial(reduce_kernel, steps, heads),
        out_shape=jax.ShapeDtypeStruct((tall, tile), jnp.bfloat16),
        in_specs=[vmem, vmem, vmem, anywhere],
        out_specs=vmem,
        scratch_shapes=[
            pltpu.VMEM((half, 2, members, rows), jnp.float32),
            pltpu.VMEM((128, 256), jnp.float32),
            pltpu.VMEM((members, rows, latent), jnp.bfloat16),
            pltpu.VMEM((Z,) + chunk, jnp.bfloat16),
            pltpu.VMEM((Z,) + chunk, jnp.float32),
            pltpu.VMEM((Z,) + chunk, jnp.bfloat16),
            pltpu.VMEM((Z,) + chunk, jnp.bfloat16),
            pltpu.VMEM((Z,) + chunk, jnp.bfloat16),
            pltpu.VMEM((Z,) + chunk, jnp.bfloat16),
            pltpu.VMEM(chunk, jnp.bfloat16),
            pltpu.VMEM(chunk[1:], jnp.bfloat16),
            pltpu.VMEM(w_o.shape, jnp.bfloat16),
            pltpu.VMEM((C, tiles, half * steps, tile), jnp.float32),
            pltpu.VMEM((tiles, half * steps, tile), jnp.float32),
            pltpu.VMEM((half, tall, tile), jnp.float32),
            pltpu.VMEM((half, tall, tile), jnp.bfloat16),
            pltpu.VMEM((half - 1, tall, tile), jnp.bfloat16),
            dma((half,)), dma((half,)),
            dma((Z,)), dma((Z,)), dma((Z,)), dma((Z,)), dma((Z,)), dma((Z,)),
            dma, dma,
            dma, dma((tiles,)), dma((tiles,)), dma((half,)), dma((half,)),
        ],
        compiler_params=pltpu.CompilerParams(
            collective_id=1, has_side_effects=True, vmem_limit_bytes=56 * MIB
        ),
        name="reduce_partials",
    )(partial, stat_rows, w_uv, w_o)
    out = out[: tiles * steps].reshape(tiles, steps, tile).transpose(1, 0, 2)
    return out.reshape(1, steps, model)


def move_keys(
    prefill_blocks,
    block_owner,
    block_position,
    cache_len,
    query_nope,
    query_rope,
    w_uk,
    w_uv,
    w_o,
    new_latent,
):
    members = lax.axis_size("wide")
    local_slots = prefill_blocks.shape[0]
    block_tok = prefill_blocks.shape[1]
    key_width = prefill_blocks.shape[2]
    latent = w_uk.shape[2]
    per_peer = (local_slots + members - 1) // members
    channels = members * per_peer
    is_live = block_owner >= 0
    target = jnp.where(is_live, block_owner, members)
    slot_order = jnp.arange(local_slots)
    same_peer = (target[:, None] == target[None, :]) & (slot_order[None, :] < slot_order[:, None])
    peer_rank = jnp.sum(same_peer.astype(jnp.int32), axis=1)
    slot_of = jnp.where(is_live, target * per_peer + peer_rank, channels)
    matches = slot_of[None, :] == jnp.arange(channels)[:, None]
    source_row = jnp.sum(jnp.where(matches, slot_order[None, :], 0), axis=1)
    filled = jnp.any(matches, axis=1)
    outgoing = jnp.where(
        filled[:, None, None], prefill_blocks[source_row], jnp.zeros((), prefill_blocks.dtype)
    )
    tag_values = jnp.where(filled, block_position[source_row] + 1, 0).astype(jnp.bfloat16)
    q_latent = jnp.einsum(
        "rshn,hnc->rshc", query_nope, w_uk, preferred_element_type=jnp.float32
    ).astype(jnp.bfloat16)
    query_full = jnp.concatenate([q_latent, query_rope], axis=3)
    step_count = query_full.shape[1]
    heads_here = query_full.shape[2]
    heads_all = members * heads_here
    incoming, arrived = (
        lax.all_to_all(outgoing, "wide", split_axis=0, concat_axis=0, tiled=True),
        lax.all_to_all(tag_values, "wide", split_axis=0, concat_axis=0, tiled=True),
    )
    gathered = lax.all_to_all(query_full, "wide", split_axis=0, concat_axis=2, tiled=True)
    query_rows = gathered.reshape(step_count * heads_all, key_width)
    my_len = cache_len[0]
    position = arrived.astype(jnp.int32)
    tokens = jnp.arange(block_tok)
    is_valid = (position[:, None] > 0) & (
        (position[:, None] - 1) * block_tok + tokens[None, :] < my_len
    )
    score_scale = (query_nope.shape[3] + query_rope.shape[3]) ** (-0.5)
    flat_keys = incoming.reshape(-1, key_width)
    flat_valid = is_valid.reshape(-1)
    block_rows = math.gcd(flat_keys.shape[0], 1024)
    key_blocks = flat_keys.reshape(-1, block_rows, key_width)
    valid_blocks = flat_valid.reshape(-1, block_rows)
    total_rows = query_rows.shape[0]

    def absorb(carry, key_rows, key_mask):
        running_max, weight_total, summed = carry
        scores = (
            lax.dot_general(
                query_rows, key_rows, (((1,), (1,)), ((), ())), preferred_element_type=jnp.float32
            )
            * score_scale
        )
        scores = jnp.where(key_mask, scores, -1e30)
        fresh_max = jnp.maximum(running_max, jnp.max(scores, axis=1))
        weights = jnp.where(key_mask, jnp.exp(scores - fresh_max[:, None]), 0.0)
        factor = jnp.exp(running_max - fresh_max)
        weight_total = weight_total * factor + jnp.sum(weights, axis=1)
        summed = summed * factor[:, None] + jnp.dot(
            weights.astype(jnp.bfloat16), key_rows[:, :latent], preferred_element_type=jnp.float32
        )
        return (fresh_max, weight_total, summed)

    def scan_step(carry, inputs):
        return (absorb(carry, inputs[0], inputs[1][None, :]), None)

    start_state = (
        jnp.full((total_rows,), -1e30, jnp.float32),
        jnp.zeros((total_rows,), jnp.float32),
        jnp.zeros((total_rows, latent), jnp.float32),
    )
    state, _ = lax.scan(scan_step, start_state, (key_blocks, valid_blocks))
    fresh_keys = new_latent[0]
    causal_mask = (jnp.arange(total_rows) // heads_all)[:, None] >= jnp.arange(step_count)[None, :]
    running_max, weight_total, summed = absorb(state, fresh_keys, causal_mask)
    latent_out = (
        (summed / weight_total[:, None])
        .astype(jnp.bfloat16)
        .reshape(1, step_count, heads_all, latent)
    )
    returned = lax.all_to_all(latent_out, "wide", split_axis=2, concat_axis=0, tiled=True)
    values = jnp.einsum(
        "rshc,hcv->rshv", returned, w_uv, preferred_element_type=jnp.float32
    ).astype(jnp.bfloat16)
    values = values.reshape(members, step_count, -1)
    layer_out = lax.psum_scatter(
        jnp.einsum("rsk,kd->rsd", values, w_o, preferred_element_type=jnp.float32),
        "wide",
        scatter_dimension=0,
        tiled=True,
    )
    return layer_out.astype(jnp.bfloat16)


def solution(mesh):
    in_specs = (
        P(("groups", "wide"), None, None),
        P(("groups", "wide")),
        P(("groups", "wide")),
        P(("groups", "wide")),
        P("groups", None, "wide", None),
        P("groups", None, "wide", None),
        P("wide", None, None),
        P("wide", None, None),
        P("wide", None),
        P(("groups", "wide"), None, None),
    )
    per_device = move_queries if mesh.shape["wide"] == Z * Y * C else move_keys
    out_specs = P(("groups", "wide"), None, None)
    return jax.shard_map(
        per_device, mesh=mesh, in_specs=in_specs, out_specs=out_specs, check_vma=False
    )
```

```python
import functools
import math

import jax
import jax.numpy as jnp
from jax import lax
from jax.experimental import pallas as pl
from jax.experimental.pallas import tpu as pltpu
from jax.sharding import PartitionSpec as P

MIB = 1024 * 1024
Z, Y, C = 4, 2, 2
LOW = -1e30


def place():
    me = lax.axis_index("wide")
    return me, me // (Y * C), (me // C) % Y, me % C


def at(z, y, c):
    return {"wide": (z * Y + y) * C + c}


def remote(src, dst, send, recv, device):
    return pltpu.make_async_remote_copy(
        src_ref=src,
        dst_ref=dst,
        send_sem=send,
        recv_sem=recv,
        device_id=device,
        device_id_type=pl.DeviceIdType.MESH,
    )


def greet(c, chip):
    barrier = pltpu.get_barrier_semaphore()
    others = [(lax.rem(chip + d, Z * Y)) * C + c for d in range(1, Z * Y)]
    others.append(chip * C + 1 - c)
    for other in others:
        pl.semaphore_signal(
            barrier, inc=1, device_id={"wide": other}, device_id_type=pl.DeviceIdType.MESH
        )
    pl.semaphore_wait(barrier, len(others))


PHASES = 4


def attend_kernel(
    scale, steps, heads, q_own, blocks, meta, fresh_ref, o_ref, m_ref,
    q_all, mine, theirs, metas, tags, keys,
    local_sem, send_up, send_dn, send_y, recv_up, recv_dn, recv_y,
    q_send, q_recv, key_send, key_recv, meta_send, meta_recv,
):
    me, z, y, c = place()
    chip = me // C
    chips = Z * Y
    sibling = at(z, y, 1 - c)
    load = pltpu.make_async_copy(blocks, mine, local_sem.at[0])
    load.start()
    own_local = pltpu.make_async_copy(q_own.at[c], q_all.at[me], local_sem.at[1])
    own_local.start()
    meta_local = pltpu.make_async_copy(meta, metas.at[chip], local_sem.at[2])
    meta_local.start()
    greet(c, chip)
    groups, rows, _ = q_all.shape
    piece = rows // PHASES
    per = steps * heads
    tok = mine.shape[2]
    latent = o_ref.shape[2]

    def row(zs, ys, cc):
        return (zs * Y + ys) * C + (c if cc == 0 else 1 - c)

    def cut(ref, r, g):
        return ref.at[r, pl.ds(g * piece, piece)]

    def to_sib(g):
        return remote(
            cut(q_own, 1 - c, g), cut(q_all, me, g), q_send.at[g], q_recv.at[g], sibling
        )

    def source(d, cc, r, g):
        return cut(q_own, c, g) if d == 0 and cc == 0 else cut(q_all, r, g)

    def up(d, cc, g, device=None):
        r = row(z - d, y, cc)
        i = cc * PHASES + g
        return remote(
            source(d, cc, r, g), cut(q_all, r, g), send_up.at[d, i], recv_up.at[d, i],
            at(z + 1, y, c) if device is None else device,
        )

    def dn(d, cc, g, device=None):
        r = row(z + d, y, cc)
        i = cc * PHASES + g
        return remote(
            source(d, cc, r, g), cut(q_all, r, g), send_dn.at[d, i], recv_dn.at[d, i],
            at(z - 1, y, c) if device is None else device,
        )

    def across(zs, cc, g, own=False):
        r = row(zs, y, cc)
        i = cc * PHASES + g
        return remote(
            source(0 if own else 1, cc, r, g), cut(q_all, r, g),
            send_y.at[zs, i], recv_y.at[zs, i], at(z, 1 - y, c),
        )

    def arrived(ref, r, g, send, recv):
        remote(cut(q_all, r, g), cut(q_all, r, g), send, recv, sibling).wait_recv()

    meta_copies = []
    for d in range(1, chips):
        meta_copies.append(
            remote(
                meta, metas.at[chip], meta_send.at[d], meta_recv.at[d],
                {"wide": lax.rem(chip + d, chips) * C + c},
            )
        )
    meta_copies.append(remote(meta, metas.at[chips], meta_send.at[0], meta_recv.at[0], sibling))
    key_copy = remote(blocks, theirs, key_send, key_recv, sibling)

    def send_own(cc, g):
        if cc == 1:
            to_sib(g).wait_recv()
        pl.when(z < Z - 1)(lambda: up(0, cc, g).start())
        pl.when(z > 0)(lambda: dn(0, cc, g).start())
        across(z, cc, g, True).start()

    def forward(d, g):
        for cc in range(2):
            i = cc * PHASES + g

            @pl.when(z - d >= 0)
            def _():
                r = row(z - d, y, cc)
                arrived(q_all, r, g, send_up.at[d - 1, i], recv_up.at[d - 1, i])
                if d < Z - 1:
                    pl.when(z < Z - 1)(lambda: up(d, cc, g).start())
                across(z - d, cc, g).start()

            @pl.when(z + d < Z)
            def _():
                r = row(z + d, y, cc)
                arrived(q_all, r, g, send_dn.at[d - 1, i], recv_dn.at[d - 1, i])
                if d < Z - 1:
                    pl.when(z > 0)(lambda: dn(d, cc, g).start())
                across(z + d, cc, g).start()

    def arrive_y(g):
        for zs in range(Z):
            for cc in range(2):
                i = cc * PHASES + g
                arrived(q_all, row(zs, 1 - y, cc), g, send_y.at[zs, i], recv_y.at[zs, i])

    for g in range(PHASES):
        to_sib(g).start()
    for copy in meta_copies:
        copy.start()
    send_own(0, 0)
    send_own(1, 0)
    key_copy.start()
    for g in range(1, PHASES):
        send_own(0, g)
        send_own(1, g)
    forward(1, 0)
    forward(2, 0)
    forward(3, 0)

    keys[:, 8 * tok :] = fresh_ref[...]
    lane = lax.broadcasted_iota(jnp.int32, (1, tok), 1)
    count = groups * per
    lane_all = lax.broadcasted_iota(jnp.int32, (count, tok), 1)
    step_of = (lax.broadcasted_iota(jnp.int32, (count, tok), 0) % per) // heads
    meta_local.wait()
    for copy in meta_copies:
        copy.wait_recv()
    tag_copy = pltpu.make_async_copy(metas, tags, local_sem.at[3])
    tag_copy.start()
    tag_copy.wait()
    load.wait()
    key_copy.wait_recv()
    own_local.wait()

    def attend(g, u):
        k = g * 2 + u
        query = q_all[:, g * piece : (g + 1) * piece].astype(jnp.float32)
        query = query[:, u * per : (u + 1) * per].reshape(count, -1).astype(jnp.bfloat16)
        length = tags[k, 1, 0]
        limits = []
        half = tags.shape[2] // 2
        for side, (held, tag) in enumerate(((mine, chip), (theirs, chips))):
            for s in range(4):
                spot = (k * C + c) * 4 + s
                index = tags[tag, 0, spot]
                position = tags[tag, 0, half + spot]
                limits.append(jnp.where(position > 0, length - (position - 1) * tok, 0))
                at_col = (side * 4 + s) * tok
                keys[:, at_col : at_col + tok] = held[index]
        scores = jnp.dot(query, keys[...], preferred_element_type=jnp.float32) * scale
        parts = []
        for s in range(8):
            parts.append(jnp.where(lane < limits[s], scores[:, s * tok : (s + 1) * tok], LOW))
        bound = jnp.where(k == chip, step_of, -1)
        parts.append(jnp.where(lane_all <= bound, scores[:, 8 * tok :], LOW))
        masked = jnp.concatenate(parts, axis=1)
        top = jnp.maximum(jnp.max(masked, axis=1, keepdims=True), -1e29)
        weights = jnp.exp(masked - top)
        total = jnp.sum(weights, axis=1, keepdims=True)
        out = lax.dot_general(
            weights.astype(jnp.bfloat16),
            keys[:latent, :],
            (((1,), (1,)), ((), ())),
            preferred_element_type=jnp.float32,
        )
        stat = jnp.where(lane_all == 0, top, total)
        return out.reshape(groups, per, latent), stat.reshape(groups, per, tok)

    def put(g, first, second):
        span = slice(g * piece, (g + 1) * piece)
        o_ref[:, span] = jnp.concatenate([first[0], second[0]], axis=1).astype(jnp.bfloat16)
        m_ref[:, span] = jnp.concatenate([first[1], second[1]], axis=1)

    for g in range(PHASES):
        if g + 1 < PHASES:
            forward(1, g + 1)
        arrive_y(g)
        first = attend(g, 0)
        if g + 1 < PHASES:
            forward(2, g + 1)
        second = attend(g, 1)
        if g + 1 < PHASES:
            forward(3, g + 1)
        put(g, first, second)

    for g in range(PHASES):
        to_sib(g).wait_send()
        for cc in range(2):
            for zs in range(Z):
                across(zs, cc, g).wait_send()
            for d in range(Z - 1):
                pl.when((z - d >= 0) & (z < Z - 1))(lambda: up(d, cc, g).wait_send())
                pl.when((z + d < Z) & (z > 0))(lambda: dn(d, cc, g).wait_send())
    key_copy.wait_send()
    for copy in meta_copies:
        copy.wait_send()


def reduce_kernel(
    steps, heads, o_ref, stat_ref, w_uv_ref, w_o_ref, out_ref,
    stats, square, scaled, y_in, acc, up_in, dn_in, up_out, dn_out, fin, sib_in,
    w_o, part, part_in, rows_f, message, inbox,
    stat_send, stat_recv, send_y, recv_y, send_up, recv_up, send_dn, recv_dn, sib_send, sib_recv,
    load_sem, part_send, part_recv, row_send, row_recv,
):
    me, z, y, c = place()
    chip = me // C
    greet(c, chip)
    chips = Z * Y
    stat_copies = []
    for d in range(1, chips):
        copy = remote(
            stat_ref, stats.at[d], stat_send.at[d], stat_recv.at[d],
            {"wide": lax.rem(chip + d, chips) * C + c},
        )
        copy.start()
        stat_copies.append(copy)
    load = pltpu.make_async_copy(w_o_ref, w_o, load_sem)
    load.start()
    groups = stat_ref.shape[1]
    width = o_ref.shape[1]
    square[...] = jnp.zeros_like(square)
    stats[0] = stat_ref[...]
    for copy in stat_copies:
        copy.wait_recv()
    top = stats[0, 0]
    for d in range(1, chips):
        top = jnp.maximum(top, stats[d, 0])
    total = jnp.zeros_like(top)
    for d in range(chips):
        total += stats[d, 1] * jnp.exp(stats[d, 0] - top)
    square[:groups, :width] = jnp.exp(stats[0, 0] - top) / total
    square_t = square[...].T

    f_all = square_t[:width, :groups]

    def scale_chunk(base):
        for cc in range(C):
            j = base + cc
            lanes = lax.broadcasted_iota(jnp.int32, f_all.shape, 1)
            factor = jnp.sum(jnp.where(lanes == j, f_all, 0.0), axis=1, keepdims=True)
            scaled[j] = (o_ref[j].astype(jnp.float32) * factor).astype(jnp.bfloat16)

    order = (3, 0, 2, 1)

    def y_copy(t):
        base = (t * Y + 1 - y) * C
        return remote(
            scaled.at[pl.ds(base, C)], y_in.at[t], send_y.at[t], recv_y.at[t], at(z, 1 - y, c)
        )

    for t in order:
        scale_chunk((t * Y + 1 - y) * C)
        y_copy(t).start()
    for t in order:
        scale_chunk((t * Y + y) * C)

    def up_copy(t):
        return remote(
            up_out.at[t], up_in.at[t], send_up.at[t], recv_up.at[t], at(z + 1, y, c)
        )

    def dn_copy(t):
        return remote(
            dn_out.at[t], dn_in.at[t], send_dn.at[t], recv_dn.at[t], at(z - 1, y, c)
        )

    def up_arrived(t):
        remote(
            up_out.at[t], up_in.at[t], send_up.at[t], recv_up.at[t], at(z, y, 1 - c)
        ).wait_recv()

    def dn_arrived(t):
        remote(
            dn_out.at[t], dn_in.at[t], send_dn.at[t], recv_dn.at[t], at(z, y, 1 - c)
        ).wait_recv()

    def get_y(t):
        y_copy(t).wait_recv()
        mine = scaled[pl.ds((t * Y + y) * C, C)].astype(jnp.float32)
        acc[t] = mine + y_in[t].astype(jnp.float32)

    def send_upward(t):
        @pl.when(z == 0)
        def _():
            up_out[t] = acc[t].astype(jnp.bfloat16)

        @pl.when((z > 0) & (z < t))
        def _():
            up_arrived(t)
            up_out[t] = (acc[t] + up_in[t].astype(jnp.float32)).astype(jnp.bfloat16)

        pl.when(z < t)(lambda: up_copy(t).start())

    def send_downward(t):
        @pl.when(z == Z - 1)
        def _():
            dn_out[t] = acc[t].astype(jnp.bfloat16)

        @pl.when((z < Z - 1) & (z > t))
        def _():
            dn_arrived(t)
            dn_out[t] = (acc[t] + dn_in[t].astype(jnp.float32)).astype(jnp.bfloat16)

        pl.when(z > t)(lambda: dn_copy(t).start())

    get_y(3)
    send_upward(3)
    get_y(0)
    send_downward(0)
    get_y(2)
    send_upward(2)
    get_y(1)
    send_downward(1)
    send_upward(1)
    send_downward(2)
    for t in range(Z):

        @pl.when(z == t)
        def _():
            value = acc[t]
            if t > 0:
                up_arrived(t)
                value = value + up_in[t].astype(jnp.float32)
            if t < Z - 1:
                dn_arrived(t)
                value = value + dn_in[t].astype(jnp.float32)
            fin[...] = value.astype(jnp.bfloat16)

    swap = remote(fin.at[1 - c], sib_in, sib_send, sib_recv, at(z, y, 1 - c))
    swap.start()
    per = chips * steps
    swap.wait()
    even = jnp.where(c == 0, fin[c], sib_in[...])
    odd = jnp.where(c == 0, sib_in[...], fin[c])
    both = jnp.concatenate([even, odd], axis=0)
    row_head = lax.broadcasted_iota(jnp.int32, (both.shape[0], w_uv_ref.shape[2]), 0) % heads
    values = []
    for h in range(heads):
        every = jnp.dot(both, w_uv_ref[h], preferred_element_type=jnp.float32)
        every = jnp.where(row_head == h, every, 0.0)
        values.append(jnp.sum(every.reshape(C * per, heads, -1), axis=1))
    values = jnp.concatenate(values, axis=1).astype(jnp.bfloat16)
    rows_f[...] = jnp.zeros_like(rows_f)
    load.wait()
    tiles, _, wide = part_in.shape

    def part_copy(i):
        return remote(
            part.at[1 - c, i], part_in.at[i], part_send.at[i], part_recv.at[i], at(z, y, 1 - c)
        )

    for i in range(tiles):
        share = jnp.dot(
            values, w_o[:, i * wide : (i + 1) * wide], preferred_element_type=jnp.float32
        )
        part[0, i] = share[:per]
        part[1, i] = share[per:]
        part_copy(i).start()
    for i in range(tiles):
        part_copy(i).wait_recv()
        summed = part[c, i] + part_in[i]
        for k in range(chips):
            rows_f[k, i * steps : (i + 1) * steps, :] = summed[k * steps : (k + 1) * steps]
    message[...] = rows_f[...].astype(jnp.bfloat16)
    row_copies = []
    for d in range(1, chips):
        other = lax.rem(chip + d, chips)
        copy = remote(
            message.at[other], inbox.at[d - 1], row_send.at[d - 1], row_recv.at[d - 1],
            {"wide": other * C + c},
        )
        copy.start()
        row_copies.append(copy)
    result = rows_f[chip]
    for d in range(1, chips):
        row_copies[d - 1].wait_recv()
        result = result + inbox[d - 1].astype(jnp.float32)
    out_ref[...] = result.astype(jnp.bfloat16)
    for i in range(tiles):
        part_copy(i).wait_send()
    for copy in row_copies:
        copy.wait_send()
    for t in range(Z):
        y_copy(t).wait_send()
        pl.when(z < t)(lambda: up_copy(t).wait_send())
        pl.when(z > t)(lambda: dn_copy(t).wait_send())
    for copy in stat_copies:
        copy.wait_send()


def move_queries(
    prefill_blocks, block_owner, block_position, cache_len,
    query_nope, query_rope, w_uk, w_uv, w_o, new_latent,
):
    members = lax.axis_size("wide")
    slots, tok, width = prefill_blocks.shape
    latent = w_uk.shape[2]
    requests, steps, heads = query_nope.shape[:3]
    per = steps * heads
    half = members // C
    rows = half * per
    per_peer = (slots + members - 1) // members
    blocks_t = jnp.swapaxes(prefill_blocks, 1, 2)
    me, z, y, c = place()
    chip = me // C
    scale = (query_nope.shape[3] + query_rope.shape[3]) ** (-0.5)

    order = jnp.arange(slots)
    same = (block_owner[:, None] == block_owner[None, :]) & (order[None, :] < order[:, None])
    rank = jnp.sum(same.astype(jnp.int32), axis=1)
    slot_of = jnp.where(block_owner >= 0, block_owner * per_peer + rank, members * per_peer)
    matches = slot_of[None, :] == jnp.arange(members * per_peer)[:, None]
    source = jnp.sum(jnp.where(matches, order[None, :], 0), axis=1)
    place_of = jnp.sum(jnp.where(matches, block_position[None, :] + 1, 0), axis=1)
    channels = members * per_peer
    meta = jnp.concatenate(
        [
            jnp.concatenate([source, place_of])[None, :],
            jnp.broadcast_to(cache_len[:1, None], (7, 2 * channels)),
        ]
    ).astype(jnp.int32)

    q_latent = jnp.einsum(
        "rshn,hnc->rshc", query_nope, w_uk, preferred_element_type=jnp.float32
    ).astype(jnp.bfloat16)
    q_full = jnp.concatenate([q_latent, query_rope], axis=3)
    q_own = q_full.reshape(half, C, per, width).transpose(1, 0, 2, 3).reshape(C, rows, width)

    anywhere = pl.BlockSpec(memory_space=pl.ANY)
    vmem = pl.BlockSpec(memory_space=pltpu.VMEM)
    dma = pltpu.SemaphoreType.DMA
    fresh = jnp.zeros((width, tok), jnp.bfloat16).at[:, :steps].set(new_latent[0].T)
    pieces = 2 * PHASES
    partial, stat = pl.pallas_call(
        functools.partial(attend_kernel, scale, steps, heads),
        out_shape=(
            jax.ShapeDtypeStruct((members, rows, latent), jnp.bfloat16),
            jax.ShapeDtypeStruct((members, rows, tok), jnp.float32),
        ),
        in_specs=[anywhere, anywhere, anywhere, vmem],
        out_specs=(vmem, vmem),
        scratch_shapes=[
            pltpu.VMEM((members, rows, width), jnp.bfloat16),
            pltpu.VMEM(blocks_t.shape, jnp.bfloat16),
            pltpu.VMEM(blocks_t.shape, jnp.bfloat16),
            pltpu.VMEM((half + 1,) + meta.shape, jnp.int32),
            pltpu.SMEM((half + 1,) + meta.shape, jnp.int32),
            pltpu.VMEM((width, (2 * per_peer + 1) * tok), jnp.bfloat16),
            dma((4,)),
            dma((Z, pieces)), dma((Z, pieces)), dma((Z, pieces)),
            dma((Z, pieces)), dma((Z, pieces)), dma((Z, pieces)),
            dma((PHASES,)), dma((PHASES,)), dma, dma, dma((half,)), dma((half,)),
        ],
        compiler_params=pltpu.CompilerParams(
            collective_id=0, has_side_effects=True, vmem_limit_bytes=56 * MIB
        ),
        name="gather_and_attend",
    )(q_own, blocks_t, meta, fresh)
    stat_rows = stat[:, :, :2].transpose(2, 0, 1)

    chunk = (C, rows, latent)
    model = w_o.shape[1]
    tile = math.gcd(model, 512)
    tiles = model // tile
    tall = (tiles * steps + 15) // 16 * 16
    out = pl.pallas_call(
        functools.partial(reduce_kernel, steps, heads),
        out_shape=jax.ShapeDtypeStruct((tall, tile), jnp.bfloat16),
        in_specs=[vmem, vmem, vmem, anywhere],
        out_specs=vmem,
        scratch_shapes=[
            pltpu.VMEM((half, 2, members, rows), jnp.float32),
            pltpu.VMEM((128, 256), jnp.float32),
            pltpu.VMEM((members, rows, latent), jnp.bfloat16),
            pltpu.VMEM((Z,) + chunk, jnp.bfloat16),
            pltpu.VMEM((Z,) + chunk, jnp.float32),
            pltpu.VMEM((Z,) + chunk, jnp.bfloat16),
            pltpu.VMEM((Z,) + chunk, jnp.bfloat16),
            pltpu.VMEM((Z,) + chunk, jnp.bfloat16),
            pltpu.VMEM((Z,) + chunk, jnp.bfloat16),
            pltpu.VMEM(chunk, jnp.bfloat16),
            pltpu.VMEM(chunk[1:], jnp.bfloat16),
            pltpu.VMEM(w_o.shape, jnp.bfloat16),
            pltpu.VMEM((C, tiles, half * steps, tile), jnp.float32),
            pltpu.VMEM((tiles, half * steps, tile), jnp.float32),
            pltpu.VMEM((half, tall, tile), jnp.float32),
            pltpu.VMEM((half, tall, tile), jnp.bfloat16),
            pltpu.VMEM((half - 1, tall, tile), jnp.bfloat16),
            dma((half,)), dma((half,)),
            dma((Z,)), dma((Z,)), dma((Z,)), dma((Z,)), dma((Z,)), dma((Z,)),
            dma, dma,
            dma, dma((tiles,)), dma((tiles,)), dma((half,)), dma((half,)),
        ],
        compiler_params=pltpu.CompilerParams(
            collective_id=1, has_side_effects=True, vmem_limit_bytes=56 * MIB
        ),
        name="reduce_partials",
    )(partial, stat_rows, w_uv, w_o)
    out = out[: tiles * steps].reshape(tiles, steps, tile).transpose(1, 0, 2)
    return out.reshape(1, steps, model)


def move_keys(
    prefill_blocks,
    block_owner,
    block_position,
    cache_len,
    query_nope,
    query_rope,
    w_uk,
    w_uv,
    w_o,
    new_latent,
):
    members = lax.axis_size("wide")
    local_slots = prefill_blocks.shape[0]
    block_tok = prefill_blocks.shape[1]
    key_width = prefill_blocks.shape[2]
    latent = w_uk.shape[2]
    per_peer = (local_slots + members - 1) // members
    channels = members * per_peer
    is_live = block_owner >= 0
    target = jnp.where(is_live, block_owner, members)
    slot_order = jnp.arange(local_slots)
    same_peer = (target[:, None] == target[None, :]) & (slot_order[None, :] < slot_order[:, None])
    peer_rank = jnp.sum(same_peer.astype(jnp.int32), axis=1)
    slot_of = jnp.where(is_live, target * per_peer + peer_rank, channels)
    matches = slot_of[None, :] == jnp.arange(channels)[:, None]
    source_row = jnp.sum(jnp.where(matches, slot_order[None, :], 0), axis=1)
    filled = jnp.any(matches, axis=1)
    outgoing = jnp.where(
        filled[:, None, None], prefill_blocks[source_row], jnp.zeros((), prefill_blocks.dtype)
    )
    tag_values = jnp.where(filled, block_position[source_row] + 1, 0).astype(jnp.bfloat16)
    q_latent = jnp.einsum(
        "rshn,hnc->rshc", query_nope, w_uk, preferred_element_type=jnp.float32
    ).astype(jnp.bfloat16)
    query_full = jnp.concatenate([q_latent, query_rope], axis=3)
    step_count = query_full.shape[1]
    heads_here = query_full.shape[2]
    heads_all = members * heads_here
    incoming, arrived = (
        lax.all_to_all(outgoing, "wide", split_axis=0, concat_axis=0, tiled=True),
        lax.all_to_all(tag_values, "wide", split_axis=0, concat_axis=0, tiled=True),
    )
    gathered = lax.all_to_all(query_full, "wide", split_axis=0, concat_axis=2, tiled=True)
    query_rows = gathered.reshape(step_count * heads_all, key_width)
    my_len = cache_len[0]
    position = arrived.astype(jnp.int32)
    tokens = jnp.arange(block_tok)
    is_valid = (position[:, None] > 0) & (
        (position[:, None] - 1) * block_tok + tokens[None, :] < my_len
    )
    score_scale = (query_nope.shape[3] + query_rope.shape[3]) ** (-0.5)
    flat_keys = incoming.reshape(-1, key_width)
    flat_valid = is_valid.reshape(-1)
    block_rows = math.gcd(flat_keys.shape[0], 1024)
    key_blocks = flat_keys.reshape(-1, block_rows, key_width)
    valid_blocks = flat_valid.reshape(-1, block_rows)
    total_rows = query_rows.shape[0]

    def absorb(carry, key_rows, key_mask):
        running_max, weight_total, summed = carry
        scores = (
            lax.dot_general(
                query_rows, key_rows, (((1,), (1,)), ((), ())), preferred_element_type=jnp.float32
            )
            * score_scale
        )
        scores = jnp.where(key_mask, scores, -1e30)
        fresh_max = jnp.maximum(running_max, jnp.max(scores, axis=1))
        weights = jnp.where(key_mask, jnp.exp(scores - fresh_max[:, None]), 0.0)
        factor = jnp.exp(running_max - fresh_max)
        weight_total = weight_total * factor + jnp.sum(weights, axis=1)
        summed = summed * factor[:, None] + jnp.dot(
            weights.astype(jnp.bfloat16), key_rows[:, :latent], preferred_element_type=jnp.float32
        )
        return (fresh_max, weight_total, summed)

    def scan_step(carry, inputs):
        return (absorb(carry, inputs[0], inputs[1][None, :]), None)

    start_state = (
        jnp.full((total_rows,), -1e30, jnp.float32),
        jnp.zeros((total_rows,), jnp.float32),
        jnp.zeros((total_rows, latent), jnp.float32),
    )
    state, _ = lax.scan(scan_step, start_state, (key_blocks, valid_blocks))
    fresh_keys = new_latent[0]
    causal_mask = (jnp.arange(total_rows) // heads_all)[:, None] >= jnp.arange(step_count)[None, :]
    running_max, weight_total, summed = absorb(state, fresh_keys, causal_mask)
    latent_out = (
        (summed / weight_total[:, None])
        .astype(jnp.bfloat16)
        .reshape(1, step_count, heads_all, latent)
    )
    returned = lax.all_to_all(latent_out, "wide", split_axis=2, concat_axis=0, tiled=True)
    values = jnp.einsum(
        "rshc,hcv->rshv", returned, w_uv, preferred_element_type=jnp.float32
    ).astype(jnp.bfloat16)
    values = values.reshape(members, step_count, -1)
    layer_out = lax.psum_scatter(
        jnp.einsum("rsk,kd->rsd", values, w_o, preferred_element_type=jnp.float32),
        "wide",
        scatter_dimension=0,
        tiled=True,
    )
    return layer_out.astype(jnp.bfloat16)


def solution(mesh):
    in_specs = (
        P(("groups", "wide"), None, None),
        P(("groups", "wide")),
        P(("groups", "wide")),
        P(("groups", "wide")),
        P("groups", None, "wide", None),
        P("groups", None, "wide", None),
        P("wide", None, None),
        P("wide", None, None),
        P("wide", None),
        P(("groups", "wide"), None, None),
    )
    per_device = move_queries if mesh.shape["wide"] == Z * Y * C else move_keys
    out_specs = P(("groups", "wide"), None, None)
    return jax.shard_map(
        per_device, mesh=mesh, in_specs=in_specs, out_specs=out_specs, check_vma=False
    )
```

```python
import functools
import math

import jax
import jax.numpy as jnp
from jax import lax
from jax.experimental import pallas as pl
from jax.experimental.pallas import tpu as pltpu
from jax.sharding import PartitionSpec as P

MIB = 1024 * 1024
Z, Y, C = 4, 2, 2
LOW = -1e30


def place():
    me = lax.axis_index("wide")
    return me, me // (Y * C), (me // C) % Y, me % C


def at(z, y, c):
    return {"wide": (z * Y + y) * C + c}


def remote(src, dst, send, recv, device):
    return pltpu.make_async_remote_copy(
        src_ref=src,
        dst_ref=dst,
        send_sem=send,
        recv_sem=recv,
        device_id=device,
        device_id_type=pl.DeviceIdType.MESH,
    )


def greet(c, chip):
    barrier = pltpu.get_barrier_semaphore()
    others = [(lax.rem(chip + d, Z * Y)) * C + c for d in range(1, Z * Y)]
    others.append(chip * C + 1 - c)
    for other in others:
        pl.semaphore_signal(
            barrier, inc=1, device_id={"wide": other}, device_id_type=pl.DeviceIdType.MESH
        )
    pl.semaphore_wait(barrier, len(others))


PHASES = 4


def attend_kernel(
    scale, steps, heads, q_own, blocks, meta, fresh_ref, o_ref, m_ref,
    q_all, mine, theirs, metas, tags, keys,
    local_sem, send_up, send_dn, send_y, recv_up, recv_dn, recv_y,
    q_send, q_recv, key_send, key_recv, meta_send, meta_recv,
):
    me, z, y, c = place()
    chip = me // C
    chips = Z * Y
    sibling = at(z, y, 1 - c)
    load = pltpu.make_async_copy(blocks, mine, local_sem.at[0])
    load.start()
    own_local = pltpu.make_async_copy(q_own.at[c], q_all.at[me], local_sem.at[1])
    own_local.start()
    meta_local = pltpu.make_async_copy(meta, metas.at[chip], local_sem.at[2])
    meta_local.start()
    greet(c, chip)
    groups, rows, _ = q_all.shape
    piece = rows // PHASES
    per = steps * heads
    tok = mine.shape[2]
    latent = o_ref.shape[2]

    def row(zs, ys, cc):
        return (zs * Y + ys) * C + (c if cc == 0 else 1 - c)

    def cut(ref, r, g):
        return ref.at[r, pl.ds(g * piece, piece)]

    def to_sib(g):
        return remote(
            cut(q_own, 1 - c, g), cut(q_all, me, g), q_send.at[g], q_recv.at[g], sibling
        )

    def source(d, cc, r, g):
        return cut(q_own, c, g) if d == 0 and cc == 0 else cut(q_all, r, g)

    def up(d, cc, g, device=None):
        r = row(z - d, y, cc)
        i = cc * PHASES + g
        return remote(
            source(d, cc, r, g), cut(q_all, r, g), send_up.at[d, i], recv_up.at[d, i],
            at(z + 1, y, c) if device is None else device,
        )

    def dn(d, cc, g, device=None):
        r = row(z + d, y, cc)
        i = cc * PHASES + g
        return remote(
            source(d, cc, r, g), cut(q_all, r, g), send_dn.at[d, i], recv_dn.at[d, i],
            at(z - 1, y, c) if device is None else device,
        )

    def across(zs, cc, g, own=False):
        r = row(zs, y, cc)
        i = cc * PHASES + g
        return remote(
            source(0 if own else 1, cc, r, g), cut(q_all, r, g),
            send_y.at[zs, i], recv_y.at[zs, i], at(z, 1 - y, c),
        )

    def arrived(ref, r, g, send, recv):
        remote(cut(q_all, r, g), cut(q_all, r, g), send, recv, sibling).wait_recv()

    meta_copies = []
    for d in range(1, chips):
        meta_copies.append(
            remote(
                meta, metas.at[chip], meta_send.at[d], meta_recv.at[d],
                {"wide": lax.rem(chip + d, chips) * C + c},
            )
        )
    meta_copies.append(remote(meta, metas.at[chips], meta_send.at[0], meta_recv.at[0], sibling))
    key_copy = remote(blocks, theirs, key_send, key_recv, sibling)

    def send_own(cc, g):
        if cc == 1:
            to_sib(g).wait_recv()
        pl.when(z < Z - 1)(lambda: up(0, cc, g).start())
        pl.when(z > 0)(lambda: dn(0, cc, g).start())
        across(z, cc, g, True).start()

    def forward(d, g):
        for cc in range(2):
            i = cc * PHASES + g

            @pl.when(z - d >= 0)
            def _():
                r = row(z - d, y, cc)
                arrived(q_all, r, g, send_up.at[d - 1, i], recv_up.at[d - 1, i])
                if d < Z - 1:
                    pl.when(z < Z - 1)(lambda: up(d, cc, g).start())
                across(z - d, cc, g).start()

            @pl.when(z + d < Z)
            def _():
                r = row(z + d, y, cc)
                arrived(q_all, r, g, send_dn.at[d - 1, i], recv_dn.at[d - 1, i])
                if d < Z - 1:
                    pl.when(z > 0)(lambda: dn(d, cc, g).start())
                across(z + d, cc, g).start()

    def arrive_y(g):
        for zs in range(Z):
            for cc in range(2):
                i = cc * PHASES + g
                arrived(q_all, row(zs, 1 - y, cc), g, send_y.at[zs, i], recv_y.at[zs, i])

    for g in range(PHASES):
        to_sib(g).start()
    for copy in meta_copies:
        copy.start()
    send_own(0, 0)
    send_own(1, 0)
    key_copy.start()
    for g in range(1, PHASES):
        send_own(0, g)
        send_own(1, g)
    forward(1, 0)
    forward(2, 0)
    forward(3, 0)

    keys[:, 8 * tok :] = fresh_ref[...]
    lane = lax.broadcasted_iota(jnp.int32, (1, tok), 1)
    count = groups * per
    lane_all = lax.broadcasted_iota(jnp.int32, (count, tok), 1)
    step_of = (lax.broadcasted_iota(jnp.int32, (count, tok), 0) % per) // heads
    meta_local.wait()
    for copy in meta_copies:
        copy.wait_recv()
    tag_copy = pltpu.make_async_copy(metas, tags, local_sem.at[3])
    tag_copy.start()
    tag_copy.wait()
    load.wait()
    key_copy.wait_recv()
    own_local.wait()

    def attend(g, u):
        k = g * 2 + u
        query = q_all[:, g * piece : (g + 1) * piece].astype(jnp.float32)
        query = query[:, u * per : (u + 1) * per].reshape(count, -1).astype(jnp.bfloat16)
        length = tags[k, 1, 0]
        limits = []
        half = tags.shape[2] // 2
        for side, (held, tag) in enumerate(((mine, chip), (theirs, chips))):
            for s in range(4):
                spot = (k * C + c) * 4 + s
                index = tags[tag, 0, spot]
                position = tags[tag, 0, half + spot]
                limits.append(jnp.where(position > 0, length - (position - 1) * tok, 0))
                at_col = (side * 4 + s) * tok
                keys[:, at_col : at_col + tok] = held[index]
        scores = jnp.dot(query, keys[...], preferred_element_type=jnp.float32) * scale
        parts = []
        for s in range(8):
            parts.append(jnp.where(lane < limits[s], scores[:, s * tok : (s + 1) * tok], LOW))
        bound = jnp.where(k == chip, step_of, -1)
        parts.append(jnp.where(lane_all <= bound, scores[:, 8 * tok :], LOW))
        masked = jnp.concatenate(parts, axis=1)
        top = jnp.maximum(jnp.max(masked, axis=1, keepdims=True), -1e29)
        weights = jnp.exp(masked - top)
        total = jnp.sum(weights, axis=1, keepdims=True)
        out = lax.dot_general(
            weights.astype(jnp.bfloat16),
            keys[:latent, :],
            (((1,), (1,)), ((), ())),
            preferred_element_type=jnp.float32,
        )
        stat = jnp.where(lane_all == 0, top, total)
        return out.reshape(groups, per, latent), stat.reshape(groups, per, tok)

    def put(g, first, second):
        span = slice(g * piece, (g + 1) * piece)
        o_ref[:, span] = jnp.concatenate([first[0], second[0]], axis=1).astype(jnp.bfloat16)
        m_ref[:, span] = jnp.concatenate([first[1], second[1]], axis=1)

    for g in range(PHASES):
        if g + 1 < PHASES:
            forward(1, g + 1)
        arrive_y(g)
        first = attend(g, 0)
        if g + 1 < PHASES:
            forward(2, g + 1)
        second = attend(g, 1)
        if g + 1 < PHASES:
            forward(3, g + 1)
        put(g, first, second)

    for g in range(PHASES):
        to_sib(g).wait_send()
        for cc in range(2):
            for zs in range(Z):
                across(zs, cc, g).wait_send()
            for d in range(Z - 1):
                pl.when((z - d >= 0) & (z < Z - 1))(lambda: up(d, cc, g).wait_send())
                pl.when((z + d < Z) & (z > 0))(lambda: dn(d, cc, g).wait_send())
    key_copy.wait_send()
    for copy in meta_copies:
        copy.wait_send()


def reduce_kernel(
    steps, heads, o_ref, stat_ref, w_uv_ref, w_o_ref, out_ref,
    stats, square, scaled, y_in, acc, up_in, dn_in, up_out, dn_out, fin, sib_in,
    w_o, part, part_in, rows_f, message, inbox,
    stat_send, stat_recv, send_y, recv_y, send_up, recv_up, send_dn, recv_dn, sib_send, sib_recv,
    load_sem, part_send, part_recv, row_send, row_recv,
):
    me, z, y, c = place()
    chip = me // C
    greet(c, chip)
    chips = Z * Y
    stat_copies = []
    for d in range(1, chips):
        copy = remote(
            stat_ref, stats.at[d], stat_send.at[d], stat_recv.at[d],
            {"wide": lax.rem(chip + d, chips) * C + c},
        )
        copy.start()
        stat_copies.append(copy)
    load = pltpu.make_async_copy(w_o_ref, w_o, load_sem)
    load.start()
    groups = stat_ref.shape[1]
    width = o_ref.shape[1]
    square[...] = jnp.zeros_like(square)
    stats[0] = stat_ref[...]
    for copy in stat_copies:
        copy.wait_recv()
    top = stats[0, 0]
    for d in range(1, chips):
        top = jnp.maximum(top, stats[d, 0])
    total = jnp.zeros_like(top)
    for d in range(chips):
        total += stats[d, 1] * jnp.exp(stats[d, 0] - top)
    square[:groups, :width] = jnp.exp(stats[0, 0] - top) / total
    square_t = square[...].T

    f_all = square_t[:width, :groups]

    piece = width // PHASES

    def span(g):
        return pl.ds(g * piece, piece)

    def scale_chunk(base, g):
        f_rows = f_all[g * piece : (g + 1) * piece]
        lanes = lax.broadcasted_iota(jnp.int32, f_rows.shape, 1)
        for cc in range(C):
            j = base + cc
            factor = jnp.sum(jnp.where(lanes == j, f_rows, 0.0), axis=1, keepdims=True)
            scaled[j, span(g)] = (o_ref[j, span(g)].astype(jnp.float32) * factor).astype(
                jnp.bfloat16
            )

    order = (3, 0, 2, 1)

    def y_copy(t, g):
        base = (t * Y + 1 - y) * C
        return remote(
            scaled.at[pl.ds(base, C), span(g)], y_in.at[t, :, span(g)],
            send_y.at[t, g], recv_y.at[t, g], at(z, 1 - y, c),
        )

    for g in range(PHASES):
        for t in order:
            scale_chunk((t * Y + 1 - y) * C, g)
            y_copy(t, g).start()
    for g in range(PHASES):
        for t in order:
            scale_chunk((t * Y + y) * C, g)

    def up_copy(t, g, device=None):
        return remote(
            up_out.at[t, :, span(g)], up_in.at[t, :, span(g)], send_up.at[t, g], recv_up.at[t, g],
            at(z + 1, y, c) if device is None else device,
        )

    def dn_copy(t, g, device=None):
        return remote(
            dn_out.at[t, :, span(g)], dn_in.at[t, :, span(g)], send_dn.at[t, g], recv_dn.at[t, g],
            at(z - 1, y, c) if device is None else device,
        )

    near = at(z, y, 1 - c)

    def get_y(t, g):
        y_copy(t, g).wait_recv()
        mine = scaled[pl.ds((t * Y + y) * C, C), span(g)].astype(jnp.float32)
        acc[t, :, span(g)] = mine + y_in[t, :, span(g)].astype(jnp.float32)

    def send_upward(t, g):
        @pl.when(z == 0)
        def _():
            up_out[t, :, span(g)] = acc[t, :, span(g)].astype(jnp.bfloat16)

        @pl.when((z > 0) & (z < t))
        def _():
            up_copy(t, g, near).wait_recv()
            total = acc[t, :, span(g)] + up_in[t, :, span(g)].astype(jnp.float32)
            up_out[t, :, span(g)] = total.astype(jnp.bfloat16)

        pl.when(z < t)(lambda: up_copy(t, g).start())

    def send_downward(t, g):
        @pl.when(z == Z - 1)
        def _():
            dn_out[t, :, span(g)] = acc[t, :, span(g)].astype(jnp.bfloat16)

        @pl.when((z < Z - 1) & (z > t))
        def _():
            dn_copy(t, g, near).wait_recv()
            total = acc[t, :, span(g)] + dn_in[t, :, span(g)].astype(jnp.float32)
            dn_out[t, :, span(g)] = total.astype(jnp.bfloat16)

        pl.when(z > t)(lambda: dn_copy(t, g).start())

    def by_half(low, high):
        pl.when(z < Z // 2)(low)
        pl.when(z >= Z // 2)(high)

    for g in range(PHASES):
        get_y(3, g)
        get_y(0, g)
        by_half(lambda: send_upward(3, g), lambda: send_downward(0, g))
        get_y(2, g)
        pl.when(z < Z // 2)(lambda: send_upward(2, g))
        get_y(1, g)
        by_half(lambda: send_upward(1, g), lambda: send_downward(1, g))
        pl.when(z >= Z // 2)(lambda: send_downward(2, g))
        by_half(lambda: send_downward(0, g), lambda: send_upward(3, g))
    for g in range(PHASES):
        for t in range(Z):

            @pl.when(z == t)
            def _():
                value = acc[t, :, span(g)]
                if t > 0:
                    up_copy(t, g, near).wait_recv()
                    value = value + up_in[t, :, span(g)].astype(jnp.float32)
                if t < Z - 1:
                    dn_copy(t, g, near).wait_recv()
                    value = value + dn_in[t, :, span(g)].astype(jnp.float32)
                fin[:, span(g)] = value.astype(jnp.bfloat16)

    swap = remote(fin.at[1 - c], sib_in, sib_send, sib_recv, at(z, y, 1 - c))
    swap.start()
    per = chips * steps
    swap.wait()
    even = jnp.where(c == 0, fin[c], sib_in[...])
    odd = jnp.where(c == 0, sib_in[...], fin[c])
    both = jnp.concatenate([even, odd], axis=0)
    row_head = lax.broadcasted_iota(jnp.int32, (both.shape[0], w_uv_ref.shape[2]), 0) % heads
    values = []
    for h in range(heads):
        every = jnp.dot(both, w_uv_ref[h], preferred_element_type=jnp.float32)
        every = jnp.where(row_head == h, every, 0.0)
        values.append(jnp.sum(every.reshape(C * per, heads, -1), axis=1))
    values = jnp.concatenate(values, axis=1).astype(jnp.bfloat16)
    rows_f[...] = jnp.zeros_like(rows_f)
    load.wait()
    tiles, _, wide = part_in.shape

    def part_copy(i):
        return remote(
            part.at[1 - c, i], part_in.at[i], part_send.at[i], part_recv.at[i], at(z, y, 1 - c)
        )

    for i in range(tiles):
        share = jnp.dot(
            values, w_o[:, i * wide : (i + 1) * wide], preferred_element_type=jnp.float32
        )
        part[0, i] = share[:per]
        part[1, i] = share[per:]
        part_copy(i).start()
    for i in range(tiles):
        part_copy(i).wait_recv()
        summed = part[c, i] + part_in[i]
        for k in range(chips):
            rows_f[k, i * steps : (i + 1) * steps, :] = summed[k * steps : (k + 1) * steps]
    message[...] = rows_f[...].astype(jnp.bfloat16)
    row_copies = []
    for d in range(1, chips):
        other = lax.rem(chip + d, chips)
        copy = remote(
            message.at[other], inbox.at[d - 1], row_send.at[d - 1], row_recv.at[d - 1],
            {"wide": other * C + c},
        )
        copy.start()
        row_copies.append(copy)
    result = rows_f[chip]
    for d in range(1, chips):
        row_copies[d - 1].wait_recv()
        result = result + inbox[d - 1].astype(jnp.float32)
    out_ref[...] = result.astype(jnp.bfloat16)
    for i in range(tiles):
        part_copy(i).wait_send()
    for copy in row_copies:
        copy.wait_send()
    for t in range(Z):
        for g in range(PHASES):
            y_copy(t, g).wait_send()
            pl.when(z < t)(lambda: up_copy(t, g).wait_send())
            pl.when(z > t)(lambda: dn_copy(t, g).wait_send())
    for copy in stat_copies:
        copy.wait_send()


def move_queries(
    prefill_blocks, block_owner, block_position, cache_len,
    query_nope, query_rope, w_uk, w_uv, w_o, new_latent,
):
    members = lax.axis_size("wide")
    slots, tok, width = prefill_blocks.shape
    latent = w_uk.shape[2]
    requests, steps, heads = query_nope.shape[:3]
    per = steps * heads
    half = members // C
    rows = half * per
    per_peer = (slots + members - 1) // members
    blocks_t = jnp.swapaxes(prefill_blocks, 1, 2)
    me, z, y, c = place()
    chip = me // C
    scale = (query_nope.shape[3] + query_rope.shape[3]) ** (-0.5)

    order = jnp.arange(slots)
    same = (block_owner[:, None] == block_owner[None, :]) & (order[None, :] < order[:, None])
    rank = jnp.sum(same.astype(jnp.int32), axis=1)
    slot_of = jnp.where(block_owner >= 0, block_owner * per_peer + rank, members * per_peer)
    matches = slot_of[None, :] == jnp.arange(members * per_peer)[:, None]
    source = jnp.sum(jnp.where(matches, order[None, :], 0), axis=1)
    place_of = jnp.sum(jnp.where(matches, block_position[None, :] + 1, 0), axis=1)
    channels = members * per_peer
    meta = jnp.concatenate(
        [
            jnp.concatenate([source, place_of])[None, :],
            jnp.broadcast_to(cache_len[:1, None], (7, 2 * channels)),
        ]
    ).astype(jnp.int32)

    q_latent = jnp.einsum(
        "rshn,hnc->rshc", query_nope, w_uk, preferred_element_type=jnp.float32
    ).astype(jnp.bfloat16)
    q_full = jnp.concatenate([q_latent, query_rope], axis=3)
    q_own = q_full.reshape(half, C, per, width).transpose(1, 0, 2, 3).reshape(C, rows, width)

    anywhere = pl.BlockSpec(memory_space=pl.ANY)
    vmem = pl.BlockSpec(memory_space=pltpu.VMEM)
    dma = pltpu.SemaphoreType.DMA
    fresh = jnp.zeros((width, tok), jnp.bfloat16).at[:, :steps].set(new_latent[0].T)
    pieces = 2 * PHASES
    partial, stat = pl.pallas_call(
        functools.partial(attend_kernel, scale, steps, heads),
        out_shape=(
            jax.ShapeDtypeStruct((members, rows, latent), jnp.bfloat16),
            jax.ShapeDtypeStruct((members, rows, tok), jnp.float32),
        ),
        in_specs=[anywhere, anywhere, anywhere, vmem],
        out_specs=(vmem, vmem),
        scratch_shapes=[
            pltpu.VMEM((members, rows, width), jnp.bfloat16),
            pltpu.VMEM(blocks_t.shape, jnp.bfloat16),
            pltpu.VMEM(blocks_t.shape, jnp.bfloat16),
            pltpu.VMEM((half + 1,) + meta.shape, jnp.int32),
            pltpu.SMEM((half + 1,) + meta.shape, jnp.int32),
            pltpu.VMEM((width, (2 * per_peer + 1) * tok), jnp.bfloat16),
            dma((4,)),
            dma((Z, pieces)), dma((Z, pieces)), dma((Z, pieces)),
            dma((Z, pieces)), dma((Z, pieces)), dma((Z, pieces)),
            dma((PHASES,)), dma((PHASES,)), dma, dma, dma((half,)), dma((half,)),
        ],
        compiler_params=pltpu.CompilerParams(
            collective_id=0, has_side_effects=True, vmem_limit_bytes=56 * MIB
        ),
        name="gather_and_attend",
    )(q_own, blocks_t, meta, fresh)
    stat_rows = stat[:, :, :2].transpose(2, 0, 1)

    chunk = (C, rows, latent)
    model = w_o.shape[1]
    tile = math.gcd(model, 512)
    tiles = model // tile
    tall = (tiles * steps + 15) // 16 * 16
    out = pl.pallas_call(
        functools.partial(reduce_kernel, steps, heads),
        out_shape=jax.ShapeDtypeStruct((tall, tile), jnp.bfloat16),
        in_specs=[vmem, vmem, vmem, anywhere],
        out_specs=vmem,
        scratch_shapes=[
            pltpu.VMEM((half, 2, members, rows), jnp.float32),
            pltpu.VMEM((128, 256), jnp.float32),
            pltpu.VMEM((members, rows, latent), jnp.bfloat16),
            pltpu.VMEM((Z,) + chunk, jnp.bfloat16),
            pltpu.VMEM((Z,) + chunk, jnp.float32),
            pltpu.VMEM((Z,) + chunk, jnp.bfloat16),
            pltpu.VMEM((Z,) + chunk, jnp.bfloat16),
            pltpu.VMEM((Z,) + chunk, jnp.bfloat16),
            pltpu.VMEM((Z,) + chunk, jnp.bfloat16),
            pltpu.VMEM(chunk, jnp.bfloat16),
            pltpu.VMEM(chunk[1:], jnp.bfloat16),
            pltpu.VMEM(w_o.shape, jnp.bfloat16),
            pltpu.VMEM((C, tiles, half * steps, tile), jnp.float32),
            pltpu.VMEM((tiles, half * steps, tile), jnp.float32),
            pltpu.VMEM((half, tall, tile), jnp.float32),
            pltpu.VMEM((half, tall, tile), jnp.bfloat16),
            pltpu.VMEM((half - 1, tall, tile), jnp.bfloat16),
            dma((half,)), dma((half,)),
            *([dma((Z, PHASES))] * 6),
            dma, dma,
            dma, dma((tiles,)), dma((tiles,)), dma((half,)), dma((half,)),
        ],
        compiler_params=pltpu.CompilerParams(
            collective_id=1, has_side_effects=True, vmem_limit_bytes=56 * MIB
        ),
        name="reduce_partials",
    )(partial, stat_rows, w_uv, w_o)
    out = out[: tiles * steps].reshape(tiles, steps, tile).transpose(1, 0, 2)
    return out.reshape(1, steps, model)


def move_keys(
    prefill_blocks,
    block_owner,
    block_position,
    cache_len,
    query_nope,
    query_rope,
    w_uk,
    w_uv,
    w_o,
    new_latent,
):
    members = lax.axis_size("wide")
    local_slots = prefill_blocks.shape[0]
    block_tok = prefill_blocks.shape[1]
    key_width = prefill_blocks.shape[2]
    latent = w_uk.shape[2]
    per_peer = (local_slots + members - 1) // members
    channels = members * per_peer
    is_live = block_owner >= 0
    target = jnp.where(is_live, block_owner, members)
    slot_order = jnp.arange(local_slots)
    same_peer = (target[:, None] == target[None, :]) & (slot_order[None, :] < slot_order[:, None])
    peer_rank = jnp.sum(same_peer.astype(jnp.int32), axis=1)
    slot_of = jnp.where(is_live, target * per_peer + peer_rank, channels)
    matches = slot_of[None, :] == jnp.arange(channels)[:, None]
    source_row = jnp.sum(jnp.where(matches, slot_order[None, :], 0), axis=1)
    filled = jnp.any(matches, axis=1)
    outgoing = jnp.where(
        filled[:, None, None], prefill_blocks[source_row], jnp.zeros((), prefill_blocks.dtype)
    )
    tag_values = jnp.where(filled, block_position[source_row] + 1, 0).astype(jnp.bfloat16)
    q_latent = jnp.einsum(
        "rshn,hnc->rshc", query_nope, w_uk, preferred_element_type=jnp.float32
    ).astype(jnp.bfloat16)
    query_full = jnp.concatenate([q_latent, query_rope], axis=3)
    step_count = query_full.shape[1]
    heads_here = query_full.shape[2]
    heads_all = members * heads_here
    incoming, arrived = (
        lax.all_to_all(outgoing, "wide", split_axis=0, concat_axis=0, tiled=True),
        lax.all_to_all(tag_values, "wide", split_axis=0, concat_axis=0, tiled=True),
    )
    gathered = lax.all_to_all(query_full, "wide", split_axis=0, concat_axis=2, tiled=True)
    query_rows = gathered.reshape(step_count * heads_all, key_width)
    my_len = cache_len[0]
    position = arrived.astype(jnp.int32)
    tokens = jnp.arange(block_tok)
    is_valid = (position[:, None] > 0) & (
        (position[:, None] - 1) * block_tok + tokens[None, :] < my_len
    )
    score_scale = (query_nope.shape[3] + query_rope.shape[3]) ** (-0.5)
    flat_keys = incoming.reshape(-1, key_width)
    flat_valid = is_valid.reshape(-1)
    block_rows = math.gcd(flat_keys.shape[0], 1024)
    key_blocks = flat_keys.reshape(-1, block_rows, key_width)
    valid_blocks = flat_valid.reshape(-1, block_rows)
    total_rows = query_rows.shape[0]

    def absorb(carry, key_rows, key_mask):
        running_max, weight_total, summed = carry
        scores = (
            lax.dot_general(
                query_rows, key_rows, (((1,), (1,)), ((), ())), preferred_element_type=jnp.float32
            )
            * score_scale
        )
        scores = jnp.where(key_mask, scores, -1e30)
        fresh_max = jnp.maximum(running_max, jnp.max(scores, axis=1))
        weights = jnp.where(key_mask, jnp.exp(scores - fresh_max[:, None]), 0.0)
        factor = jnp.exp(running_max - fresh_max)
        weight_total = weight_total * factor + jnp.sum(weights, axis=1)
        summed = summed * factor[:, None] + jnp.dot(
            weights.astype(jnp.bfloat16), key_rows[:, :latent], preferred_element_type=jnp.float32
        )
        return (fresh_max, weight_total, summed)

    def scan_step(carry, inputs):
        return (absorb(carry, inputs[0], inputs[1][None, :]), None)

    start_state = (
        jnp.full((total_rows,), -1e30, jnp.float32),
        jnp.zeros((total_rows,), jnp.float32),
        jnp.zeros((total_rows, latent), jnp.float32),
    )
    state, _ = lax.scan(scan_step, start_state, (key_blocks, valid_blocks))
    fresh_keys = new_latent[0]
    causal_mask = (jnp.arange(total_rows) // heads_all)[:, None] >= jnp.arange(step_count)[None, :]
    running_max, weight_total, summed = absorb(state, fresh_keys, causal_mask)
    latent_out = (
        (summed / weight_total[:, None])
        .astype(jnp.bfloat16)
        .reshape(1, step_count, heads_all, latent)
    )
    returned = lax.all_to_all(latent_out, "wide", split_axis=2, concat_axis=0, tiled=True)
    values = jnp.einsum(
        "rshc,hcv->rshv", returned, w_uv, preferred_element_type=jnp.float32
    ).astype(jnp.bfloat16)
    values = values.reshape(members, step_count, -1)
    layer_out = lax.psum_scatter(
        jnp.einsum("rsk,kd->rsd", values, w_o, preferred_element_type=jnp.float32),
        "wide",
        scatter_dimension=0,
        tiled=True,
    )
    return layer_out.astype(jnp.bfloat16)


def solution(mesh):
    in_specs = (
        P(("groups", "wide"), None, None),
        P(("groups", "wide")),
        P(("groups", "wide")),
        P(("groups", "wide")),
        P("groups", None, "wide", None),
        P("groups", None, "wide", None),
        P("wide", None, None),
        P("wide", None, None),
        P("wide", None),
        P(("groups", "wide"), None, None),
    )
    per_device = move_queries if mesh.shape["wide"] == Z * Y * C else move_keys
    out_specs = P(("groups", "wide"), None, None)
    return jax.shard_map(
        per_device, mesh=mesh, in_specs=in_specs, out_specs=out_specs, check_vma=False
    )
```
